32 devices in a mesh: groups: 2 (over y), rows: 4 (over z), heads: 4 (over x, core).
Axes of the slice: x: 2, y: 2, z: 4, core: 2. Of those that a mesh axis runs over, the one named last changes fastest.
Arguments:
- resid: bfloat16 [256, 5120], P(('groups', 'heads'), 'rows'), parts along dimension 0, may hold values from -6 to 6
- queries: bfloat16 [256, 8192], P(('groups', 'rows'), 'heads'), parts along dimension 0, may hold values from -600 to 600
- kv_codes: bfloat16 [512, 2, 8, 128, 128], P(('groups', 'rows'), None, 'heads'), parts along dimension 0, may hold values from -127 to 127, as said below
- kv_scale: float32 [4, 8], P('groups', 'heads'), parts along dimension 0, may hold values from 0.004 to 0.016
- row_blocks: int32 [256, 32], P(('groups', 'rows')), parts along dimension 0, may hold values from 0 to 255, as said below
- row_len: int32 [256], P(('groups', 'rows')), parts along dimension 0, may hold values from 1 to 4096, as said below
- w_out: bfloat16 [8192, 5120], P('heads', 'rows'), may hold values from -0.0625 to 0.0625
- norm_gain: float32 [5120], replicated, may hold values from 0.1 to 1.9
- w_gate: bfloat16 [5120, 16384], P(None, ('rows', 'heads')), may hold values from -0.078125 to 0.078125
- w_up: bfloat16 [5120, 16384], P(None, ('rows', 'heads')), may hold values from -0.078125 to 0.078125
- w_down: bfloat16 [16384, 5120], P(('rows', 'heads')), may hold values from -0.0625 to 0.0625
Outputs:
- layer_out: bfloat16 [256, 5120], P(('groups', 'heads'), 'rows'), parts along dimension 0
The draws below stay inside these ranges and needn't reach their ends.
There are 2 independent parts, one for each index of `groups`. The reference program is written for one: setup_inputs(seed, part) draws one part's arguments, and reference() takes and returns one part's arrays. A program takes and returns all parts, laid end to end along the dimension named above; an argument that names none is the same for every part. Nothing has to cross between parts.
Inputs may be any that keep to these rules, and one draw needn't show every extreme that they name: `row_blocks`: each row's list holds the 32 distinct block ids of one document in the document's order; all blocks of a document lie in one range from o * 64 to (o + 1) * 64 - 1 for some index o of rows, and every such range holds 2 documents. Among the rows of one index of rows (aligned blocks of 32 rows) at most 16 have lists in the same range, and exactly 16 do for some range. `row_len`: the largest value, 4096, is reached. `kv_codes`: every code is a whole number, so the codes fit int8.
All inputs are finite; a program needn't handle non-finite values.
Results may differ from the reference program's by a relative error of at most 0.015.
Values may be sent and summed in bfloat16 or wider, within the bound.
No kernel may reach another device: no remote copies, remote signals or barrier semaphores. Data moves between devices by JAX's collectives and lax.ppermute only.
A program may use at most 128 MiB of HBM per device.

```python
import math
from functools import partial
import jax
import jax.numpy as jnp
from jax import lax

D = 5120
HQ = 64
KVH = 8
HD = 128
FFW = 16384
BLK_TOK = 128
DOC_DEV = 2
BLK_DEV = 64
R_DEV = 32
R = 128
POOL = 256
LIST = 32
CAP = 16


def owners_block(subkey):
    row_devs = R // R_DEV
    key_star, key_rest, key_order = jax.random.split(subkey, 3)
    top_owner = jax.random.randint(key_star, (), 0, row_devs)
    others = jax.random.permutation(key_rest, (row_devs - 1) * CAP)[:R_DEV - CAP]
    other_owner = (others // CAP + top_owner + 1) % row_devs
    owners = jnp.concatenate([jnp.full((CAP,), top_owner, jnp.int32), other_owner.astype(jnp.int32)])
    return owners[jax.random.permutation(key_order, R_DEV)]


def block_order(subkey):
    return jax.random.permutation(subkey, BLK_DEV)


def layout_lists(key):
    row_devs = R // R_DEV
    owners = jax.vmap(owners_block)(jax.random.split(jax.random.fold_in(key, 11), row_devs)).reshape(R)
    documents = jax.random.randint(jax.random.fold_in(key, 12), (R,), 0, DOC_DEV)
    orders = jax.vmap(block_order)(jax.random.split(jax.random.fold_in(key, 13), row_devs))
    chosen = orders[owners].reshape(R, DOC_DEV, LIST)
    picked = jnp.take_along_axis(chosen, documents[:, None, None], axis=1)[:, 0]
    return (picked + owners[:, None] * BLK_DEV).astype(jnp.int32)


def drawn_codes(key):
    lead_int = jax.random.randint(jax.random.fold_in(key, 21), (POOL, KVH, HD), -127, 128)
    nudge_int = jax.random.randint(jax.random.fold_in(key, 22), (POOL, KVH, HD), -20, 21)
    follow_int = jnp.clip(lead_int + nudge_int, -127, 127)
    return (lead_int.astype(jnp.float32), follow_int.astype(jnp.float32))


def draw_row_blocks(key, part):
    return layout_lists(key)


def draw_row_len(key, part):
    blocks_used = jax.random.randint(jax.random.fold_in(key, 51), (R,), 1, LIST + 1)
    cut_off = jax.random.randint(jax.random.fold_in(key, 52), (R,), 0, BLK_TOK)
    lengths = blocks_used * BLK_TOK - cut_off
    return lengths.at[0].set(LIST * BLK_TOK).astype(jnp.int32)


def draw_kv_codes(key, part):
    codes = jax.random.randint(jax.random.fold_in(key, 31), (POOL, 2, KVH, BLK_TOK, HD), -127, 128).astype(jnp.float32)
    lead_codes, follow_codes = drawn_codes(key)
    codes = codes.at[:, 0, :, 0, :].set(lead_codes)
    codes = codes.at[:, 0, :, 1, :].set(follow_codes)
    return codes.astype(jnp.bfloat16)


def draw_queries(key, part):
    base = jnp.clip(jax.random.normal(jax.random.fold_in(key, 41), (R, KVH, HQ // KVH, HD), jnp.float32), -6.0, 6.0)
    return base.reshape(R, HQ * HD).astype(jnp.bfloat16)


def spiked(values, stream_key, source, target, shards_of, factor):
    owner, partner = [(jnp.arange(values.shape[dim]) // (values.shape[dim] // shards_of)).reshape([-1 if axis == dim else 1 for axis in range(values.ndim)]) for dim in (source, target)]
    chosen = jax.random.permutation(stream_key, shards_of)[partner]
    strong = (owner == chosen) | (owner == (partner + shards_of // 2) % shards_of)
    return jnp.where(strong, factor * values, values)


def steps_of(rng, dims, cuts, smallest, high):
    level = 1.0
    for axis_at, shards_of in cuts:
        steps = jax.random.uniform(jax.random.fold_in(jax.random.fold_in(rng, 6), axis_at), (shards_of,), jnp.float32, smallest / len(cuts), high / len(cuts))
        level = level * jnp.repeat(jnp.exp(steps), dims[axis_at] // shards_of).reshape((-1,) + (1,) * (len(dims) - 1 - axis_at))
    return level


def normal_values(own_key, dims, deviation, most, cuts=(), kind=jnp.bfloat16):
    values = deviation * jax.random.normal(own_key, dims, jnp.float32)
    if cuts:
        values = values * steps_of(own_key, dims, cuts, -0.22, 0.18)
    return jnp.clip(values, -most, most).astype(kind)


def bell_draw_with(rng, shape, width, most, cuts, heavy, kind=jnp.bfloat16):
    values = width * jax.random.normal(rng, shape, jnp.float32)
    if cuts:
        values = values * steps_of(rng, shape, cuts, -0.22, 0.18)
    return jnp.clip(spiked(values, jax.random.fold_in(rng, 3), *heavy), -most, most).astype(kind)


def setup_inputs(seed: int = 0, part: int = 0) -> dict:
    splits = jax.random.split(jax.random.key(seed), 12)
    part_keys = jax.random.split(jax.random.fold_in(splits[11], part), 12)
    return {
        "resid": normal_values(part_keys[0], (R, D), 1.0, 6.0, ((0, 4), (1, 4))),
        "queries": draw_queries(jax.random.fold_in(jax.random.fold_in(splits[11], part), 71), part),
        "kv_codes": draw_kv_codes(jax.random.fold_in(jax.random.fold_in(splits[11], part), 71), part),
        "kv_scale": jnp.clip(jnp.exp(math.log(0.016) - 1.3862944 * jax.random.uniform(part_keys[3], (2, KVH), jnp.float32) ** steps_of(part_keys[3], (2, KVH), ((1, 4),), -0.2, 0.2)), 0.004, 0.016),
        "row_blocks": draw_row_blocks(jax.random.fold_in(jax.random.fold_in(splits[11], part), 71), part),
        "row_len": draw_row_len(jax.random.fold_in(jax.random.fold_in(splits[11], part), 71), part),
        "w_out": normal_values(splits[6], (HQ * HD, D), (HQ * HD) ** -0.5, 0.0625, ((0, 4), (1, 4))),
        "norm_gain": jnp.clip(1.0 + 0.18 * jax.random.normal(splits[7], (D,), jnp.float32), 0.1, 1.9),
        "w_gate": normal_values(splits[8], (D, FFW), D ** -0.5, 0.078125, ((1, 16),)),
        "w_up": normal_values(splits[9], (D, FFW), D ** -0.5, 0.078125, ((1, 16),)),
        "w_down": bell_draw_with(splits[10], (FFW, D), FFW ** -0.5, 0.0625, ((0, 16),), (0, 1, 16, 2.0)),
    }


norm_eps = 1e-06

def attend_row(inputs, kv_codes, kv_scale):
    query_row, block_list, length = inputs
    picked = kv_codes[block_list]
    key_codes = jnp.transpose(picked[:, 0], (1, 0, 2, 3)).reshape(KVH, LIST * BLK_TOK, HD)
    value_codes = jnp.transpose(picked[:, 1], (1, 0, 2, 3)).reshape(KVH, LIST * BLK_TOK, HD)
    query_heads = query_row.reshape(KVH, HQ // KVH, HD)
    scores = jnp.einsum('kgd,ktd->kgt', query_heads.astype(jnp.float32), key_codes.astype(jnp.float32))
    scores = scores * (kv_scale[0] / math.sqrt(HD))[:, None, None]
    position = jnp.arange(LIST * BLK_TOK, dtype=jnp.int32)
    scores = jnp.where(position[None, None, :] < length, scores, -jnp.inf)
    peak_score = lax.optimization_barrier(jnp.max(scores, axis=2, keepdims=True))
    weights = jnp.exp(scores - peak_score)
    denom_sum = lax.optimization_barrier(jnp.sum(weights, axis=2))
    rounded = lax.optimization_barrier(weights.astype(jnp.bfloat16)).astype(jnp.float32)
    mixture = jnp.einsum('kgt,ktd->kgd', rounded, value_codes.astype(jnp.float32))
    mixture = mixture * kv_scale[1][:, None, None] / denom_sum[..., None]
    return mixture.astype(jnp.bfloat16).reshape(HQ * HD)

def reference(resid, queries, kv_codes, kv_scale, row_blocks, row_len, w_out, norm_gain, w_gate, w_up, w_down):
    single_row = partial(attend_row, kv_codes=kv_codes, kv_scale=kv_scale)
    attended = lax.map(single_row, (queries, row_blocks, row_len))
    attn_out = jnp.dot(attended.astype(jnp.float32), w_out.astype(jnp.float32), preferred_element_type=jnp.float32)
    hidden_state = (resid.astype(jnp.float32) + attn_out).astype(jnp.bfloat16)
    as_float = hidden_state.astype(jnp.float32)
    inverse = lax.rsqrt(lax.optimization_barrier(jnp.sum(as_float * as_float, axis=1)) / D + norm_eps)
    normed = (as_float * inverse[:, None] * norm_gain).astype(jnp.bfloat16)
    gate_proj = jnp.dot(normed.astype(jnp.float32), w_gate.astype(jnp.float32), preferred_element_type=jnp.float32)
    up_proj = jnp.dot(normed.astype(jnp.float32), w_up.astype(jnp.float32), preferred_element_type=jnp.float32)
    inner_act = (jax.nn.silu(gate_proj) * up_proj).astype(jnp.bfloat16)
    ffn_out = jnp.dot(inner_act.astype(jnp.float32), w_down.astype(jnp.float32), preferred_element_type=jnp.float32)
    return (as_float + ffn_out).astype(jnp.bfloat16)
```

```python
import functools
import math

import jax
import jax.numpy as jnp
from jax import lax
from jax.experimental import pallas as pl
from jax.experimental.pallas import tpu as pltpu
from jax.sharding import PartitionSpec as P

norm_eps = 1e-06
log2_e = 1.4426950408889634
mib = 1 << 20
lanes = 128
f32 = jnp.float32
bf16 = jnp.bfloat16

vmem = functools.partial(pl.BlockSpec, memory_space=pltpu.VMEM)
smem = functools.partial(pl.BlockSpec, memory_space=pltpu.SMEM)
hbm = functools.partial(pl.BlockSpec, memory_space=pl.ANY)


def iota(shape, dim):
    return lax.broadcasted_iota(jnp.int32, shape, dim)


def mxu(a, b, contract):
    return lax.dot_general(a, b, ((contract[:1], contract[1:]), ((), ())), preferred_element_type=f32)


def dispatch_kernel(blocks_dev, me_ref, ids_ref, len_ref, q_ref, place_ref, *send_refs):
    count = len(send_refs)
    slots = send_refs[0].shape[0]
    width = q_ref.shape[1]
    rows, listed = ids_ref.shape
    me = me_ref[0]
    ids = ids_ref[...].astype(f32)
    owner = jnp.floor((ids[:, 0:1] + 0.5) * (1.0 / blocks_dev))
    ahead = owner - me.astype(f32)
    ahead = jnp.where(ahead < 0, ahead + count, ahead)
    lane = iota((rows, lanes), 1)
    hot = jnp.where(lane.astype(f32) == ahead, 1.0, 0.0)
    lower = jnp.where(iota((rows, rows), 1) < iota((rows, rows), 0), 1.0, 0.0)
    before = mxu(lower.astype(bf16), hot.astype(bf16), (1, 0))
    rank = jnp.sum(before * hot, axis=1, keepdims=True)
    target = ahead * slots + rank
    place = jnp.where(iota((rows, count * slots), 1).astype(f32) == target, 1.0, 0.0).astype(bf16)
    place_ref[...] = place
    local = (ids - owner * blocks_dev).astype(bf16)
    eye = jnp.where(iota((listed, lanes), 0) == iota((listed, lanes), 1), 1.0, 0.0).astype(bf16)
    meta = mxu(local, eye, (1, 0))
    spread = jnp.broadcast_to(len_ref[...].astype(f32), (rows, rows))
    length = jnp.sum(
        jnp.where(iota((rows, rows), 0) == iota((rows, rows), 1), spread, 0.0), axis=1, keepdims=True
    )
    high = jnp.floor(length * (1.0 / 64))
    meta = jnp.where(lane == listed, high, meta)
    meta = jnp.where(lane == listed + 1, length - high * 64, meta)
    send = mxu(place, q_ref[...], (0, 0)).astype(bf16)
    send_meta = mxu(place, meta.astype(bf16), (0, 0)).astype(bf16)
    for s in range(count):
        send_refs[s][:, 0:width] = send[s * slots : (s + 1) * slots]
        send_refs[s][:, width : width + lanes] = send_meta[s * slots : (s + 1) * slots]


def dispatch(me, queries, row_blocks, row_len, count, slots, blocks_dev):
    rows, width = queries.shape
    outs = [jax.ShapeDtypeStruct((rows, count * slots), bf16)]
    outs += [jax.ShapeDtypeStruct((slots, width + lanes), bf16)] * count
    got = pl.pallas_call(
        functools.partial(dispatch_kernel, blocks_dev),
        out_shape=outs,
        in_specs=[smem(), vmem(), vmem(), vmem()],
        out_specs=[vmem()] * (count + 1),
        name="dispatch",
    )(me, row_blocks, row_len.reshape(1, rows), queries)
    return got[0], got[1:]


tile_rows = 16


def attend_kernel(count, listed, group, step_blocks, scale_ref, kv_ref, *refs):
    in_refs, out_refs = refs[:count], refs[count : 2 * count]
    kv, qs, os, lens, ints, scalars, kv_sem, int_sem = refs[2 * count :]
    slots = out_refs[0].shape[0]
    width = out_refs[0].shape[1]
    total = count * slots
    places = qs.shape[0]
    heads, tok, dim = kv.shape[2:]
    kv_copy = pltpu.make_async_copy(kv_ref, kv, kv_sem)
    kv_copy.start()

    meta = jnp.concatenate([r[:, width : width + lanes] for r in in_refs], axis=0).astype(f32)
    lane = iota((total, lanes), 1)
    length = jnp.sum(
        jnp.where(lane == listed, meta * 64.0, jnp.where(lane == listed + 1, meta, 0.0)), axis=1, keepdims=True
    )
    ids = jnp.where(lane < listed, meta, 0.0)
    slot = iota((total, 1), 0).astype(f32)
    valid = length > 0.0
    big = float(total)

    def first_list(mask):
        first = jnp.min(jnp.where(mask, slot, big), axis=0, keepdims=True)
        return jnp.sum(jnp.where(slot == first, ids, 0.0), axis=0, keepdims=True)

    list_a = first_list(valid)
    same_a = jnp.sum(jnp.abs(ids - list_a), axis=1, keepdims=True) == 0.0
    in_a = valid & same_a
    in_b = valid & jnp.logical_not(same_a)
    list_b = first_list(in_b)
    span = float(2 * listed * tok)
    key = jnp.where(in_a, 2 * span + length, jnp.where(in_b, span + length, 0.0))
    key = key * total + (total - 1 - slot)
    eye = iota((total, total), 0) == iota((total, total), 1)
    key_row = jnp.sum(jnp.where(eye, key, 0.0), axis=0, keepdims=True)
    len_row = jnp.sum(jnp.where(eye, length, 0.0), axis=0, keepdims=True)
    rank = jnp.sum(jnp.where(key > key_row, 1.0, 0.0), axis=0, keepdims=True)
    a_row = key_row >= 2 * span * total
    b_row = jnp.logical_and(key_row >= span * total, jnp.logical_not(a_row))
    a_count = jnp.sum(jnp.where(a_row, 1.0, 0.0), axis=1, keepdims=True)
    a_tiles = jnp.floor((a_count + (tile_rows - 1)) * (1.0 / tile_rows))
    spot = jnp.where(a_row, rank, jnp.where(b_row, rank - a_count + a_tiles * tile_rows, float(places)))
    placed = iota((places, total), 0).astype(f32) == spot
    perm = jnp.where(placed, 1.0, 0.0).astype(bf16)
    len_sorted = jnp.sum(jnp.where(placed, len_row, 0.0), axis=1, keepdims=True)
    lens[...] = jnp.broadcast_to(len_sorted, (places, lanes)).astype(jnp.int32)
    tops = jnp.sum(
        jnp.where(iota((places, lanes), 0) == iota((places, lanes), 1) * tile_rows, len_sorted, 0.0),
        axis=0,
        keepdims=True,
    )
    row = iota((8, lanes), 0)
    ints[...] = jnp.where(
        row == 0, list_a, jnp.where(row == 1, list_b, jnp.where(row == 2, tops, a_tiles))
    ).astype(jnp.int32)
    int_copy = pltpu.make_async_copy(ints, scalars, int_sem)
    int_copy.start()
    queries = jnp.concatenate([r[:, 0:width] for r in in_refs], axis=0)
    qs[...] = mxu(perm, queries, (1, 0)).astype(bf16)
    os[...] = jnp.zeros_like(os)
    int_copy.wait()
    kv_copy.wait()

    tokens = step_blocks * tok
    tall = group * tile_rows
    factors = [scale_ref[0, k] * (log2_e / math.sqrt(dim)) for k in range(heads)]
    spread = iota((tall, tokens), 1)

    def tile_body(t, _):
        top = scalars[2, t]
        doc = jnp.where(t >= scalars[3, 0], 1, 0)
        at = pl.multiple_of(t * tile_rows, tile_rows)
        spans = jnp.concatenate([lens[pl.ds(at, tile_rows), :]] * group, axis=0)[:, 0:1]
        qt = [
            jnp.concatenate(
                [qs[pl.ds(at, tile_rows), (k * group + g) * dim : (k * group + g + 1) * dim] for g in range(group)],
                axis=0,
            )
            for k in range(heads)
        ]

        def step(c, carry):
            keep = spread < spans - c * tokens
            blocks = [scalars[doc, c * step_blocks + j] for j in range(step_blocks)]
            after = []
            for k in range(heads):
                peak, denom, acc = carry[k]
                keys = jnp.concatenate([kv[b, 0, k] for b in blocks], axis=0)
                scores = mxu(qt[k], keys, (1, 1)) * factors[k]
                scores = jnp.where(keep, scores, -1e30)
                higher = jnp.maximum(peak, jnp.max(scores, axis=1, keepdims=True))
                shrink = jnp.exp2(peak - higher)
                weights = jnp.exp2(scores - higher)
                denom = denom * shrink + jnp.sum(weights, axis=1, keepdims=True)
                values = jnp.concatenate([kv[b, 1, k] for b in blocks], axis=0)
                acc = acc * shrink + mxu(weights.astype(bf16), values, (1, 0))
                after.append((higher, denom, acc))
            return tuple(after)

        start = tuple(
            (jnp.full((tall, 1), -1e30, f32), jnp.zeros((tall, 1), f32), jnp.zeros((tall, dim), f32))
            for _ in range(heads)
        )
        steps = (top + (tokens - 1)) // tokens

        @pl.when(steps > 0)
        def _():
            done = lax.fori_loop(0, steps, step, start)
            for k in range(heads):
                _, denom, acc = done[k]
                out = (acc * (scale_ref[1, k] / denom)).astype(bf16)
                for g in range(group):
                    col = (k * group + g) * dim
                    os[pl.ds(at, tile_rows), col : col + dim] = out[g * tile_rows : (g + 1) * tile_rows]

        return 0

    lax.fori_loop(0, places // tile_rows, tile_body, 0)
    out = mxu(perm, os[...], (0, 0)).astype(bf16)
    for s in range(count):
        out_refs[s][...] = out[s * slots : (s + 1) * slots]


def attend(received, kv_codes, kv_scale, listed, group):
    count = len(received)
    slots, wide = received[0].shape
    width = wide - lanes
    total = count * slots
    places = total + tile_rows
    return pl.pallas_call(
        functools.partial(attend_kernel, count, listed, group, min(8, listed)),
        out_shape=[jax.ShapeDtypeStruct((slots, width), bf16)] * count,
        in_specs=[smem(), hbm()] + [vmem()] * count,
        out_specs=[vmem()] * count,
        scratch_shapes=[
            pltpu.VMEM(kv_codes.shape, bf16),
            pltpu.VMEM((places, width), bf16),
            pltpu.VMEM((places, width), bf16),
            pltpu.VMEM((places, lanes), jnp.int32),
            pltpu.VMEM((8, lanes), jnp.int32),
            pltpu.SMEM((8, lanes), jnp.int32),
            pltpu.SemaphoreType.DMA,
            pltpu.SemaphoreType.DMA,
        ],
        compiler_params=pltpu.CompilerParams(vmem_limit_bytes=32 * mib),
        name="attend",
    )(kv_scale, kv_codes, *received)


def project_kernel(count, parts, at_ref, *refs):
    in_refs, w_ref = refs[:count], refs[count]
    own_ref, out_refs = refs[count + 1], refs[count + 2 : count + 1 + parts]
    x, y = refs[count + 1 + parts :]
    rows = in_refs[0].shape[0]
    piece = own_ref.shape[0]

    @pl.when(pl.program_id(0) == 0)
    def _():
        for s in range(count):
            source = at_ref[0] - s
            source = jnp.where(source < 0, source + count, source)
            x[pl.ds(pl.multiple_of(source * rows, rows), rows), :] = in_refs[s][...]

    y[...] = mxu(x[...], w_ref[...], (1, 0))
    for s in range(parts):
        target = at_ref[1] + s
        target = jnp.where(target >= parts, target - parts, target)
        value = y[pl.ds(pl.multiple_of(target * piece, piece), piece), :]
        if s == 0:
            own_ref[...] = value
        else:
            out_refs[s - 1][...] = value.astype(bf16)


def project(at, pieces, w_out, parts):
    count = len(pieces)
    rows, depth = pieces[0].shape
    cols = w_out.shape[1]
    tall = rows * count
    piece = tall // parts
    wide = 256 if cols % 256 == 0 else cols
    whole = pl.BlockSpec((rows, depth), lambda j: (0, 0))
    part = pl.BlockSpec((piece, wide), lambda j: (0, j))
    got = pl.pallas_call(
        functools.partial(project_kernel, count, parts),
        grid=(cols // wide,),
        out_shape=[jax.ShapeDtypeStruct((piece, cols), f32)]
        + [jax.ShapeDtypeStruct((piece, cols), bf16)] * (parts - 1),
        in_specs=[smem()] + [whole] * count + [pl.BlockSpec((depth, wide), lambda j: (0, j))],
        out_specs=[part] * parts,
        scratch_shapes=[pltpu.VMEM((tall, depth), bf16), pltpu.VMEM((tall, wide), f32)],
        compiler_params=pltpu.CompilerParams(vmem_limit_bytes=32 * mib),
        name="project",
    )(at, *pieces, w_out)
    return got[0], got[1:]


def shift(x, axis, step):
    n = lax.axis_size(axis)
    return lax.ppermute(x, axis, [(i, (i + step) % n) for i in range(n)])


def shards(
    resid, queries, kv_codes, kv_scale, row_blocks, row_len, w_out, norm_gain, w_gate, w_up, w_down
):
    row_devs = lax.axis_size("rows")
    head_devs = lax.axis_size("heads")
    rows_dev, width_q = queries.shape
    listed = row_blocks.shape[1]
    blocks_dev = kv_codes.shape[0]
    heads_dev, head_dim = kv_codes.shape[2], kv_codes.shape[4]
    group = width_q // (heads_dev * head_dim)
    capacity = max(2, 2 * rows_dev // row_devs)
    slots = -(-capacity // 16) * 16
    my_row = lax.axis_index("rows").astype(jnp.int32)
    my_head = lax.axis_index("heads").astype(jnp.int32)
    at = jnp.stack([my_row, my_head])

    place, sends = dispatch(at, queries, row_blocks, row_len, row_devs, slots, blocks_dev)
    received = [sends[0]] + [shift(sends[s], "rows", s) for s in range(1, row_devs)]
    results = attend(received, kv_codes, kv_scale, listed, group)
    back = [results[0]] + [shift(results[s], "rows", -s) for s in range(1, row_devs)]
    attended = jnp.dot(place, jnp.concatenate(back, axis=0), preferred_element_type=f32).astype(bf16)
    pieces = [attended] + [shift(attended, "rows", s) for s in range(1, row_devs)]
    own, others = project(at, pieces, w_out, head_devs)
    attn_out = own
    for s in range(1, head_devs):
        attn_out = attn_out + shift(others[s - 1], "heads", s).astype(f32)
    hidden_state = (resid.astype(f32) + attn_out).astype(bf16)

    as_float = hidden_state.astype(f32)
    cols_dev = hidden_state.shape[1]
    model_width = cols_dev * row_devs
    full_rows = lax.all_gather(hidden_state, "rows", axis=1, tiled=True)
    piece_rows = lax.all_gather(full_rows, "heads", axis=0, tiled=True).astype(f32)
    totals = jnp.sum(piece_rows * piece_rows, axis=1)
    piece_rows = (
        piece_rows * lax.rsqrt(totals / model_width + norm_eps)[:, None] * norm_gain
    ).astype(bf16)
    gate_proj = jnp.dot(piece_rows, w_gate, preferred_element_type=f32)
    up_proj = jnp.dot(piece_rows, w_up, preferred_element_type=f32)
    inner_act = (jax.nn.silu(gate_proj) * up_proj).astype(bf16)
    partial_sum = jnp.dot(inner_act, w_down, preferred_element_type=f32)
    section_sum = lax.psum_scatter(partial_sum.astype(bf16), "heads", scatter_dimension=0, tiled=True)
    ffn_out = lax.psum_scatter(section_sum, "rows", scatter_dimension=1, tiled=True).astype(f32)
    return (as_float + ffn_out).astype(bf16)


def solution(mesh):
    placed = (
        P(("groups", "heads"), "rows"),
        P(("groups", "rows"), "heads"),
        P(("groups", "rows"), None, "heads", None, None),
        P("groups", "heads"),
        P(("groups", "rows"), None),
        P(("groups", "rows")),
        P("heads", "rows"),
        P(),
        P(None, ("rows", "heads")),
        P(None, ("rows", "heads")),
        P(("rows", "heads"), None),
    )
    return jax.shard_map(
        shards,
        mesh=mesh,
        in_specs=placed,
        out_specs=P(("groups", "heads"), "rows"),
        check_vma=False,
    )
```

```python
import functools
import math

import jax
import jax.numpy as jnp
from jax import lax
from jax.experimental import pallas as pl
from jax.experimental.pallas import tpu as pltpu
from jax.sharding import PartitionSpec as P

norm_eps = 1e-06
log2_e = 1.4426950408889634
mib = 1 << 20
lanes = 128
f32 = jnp.float32
bf16 = jnp.bfloat16

vmem = functools.partial(pl.BlockSpec, memory_space=pltpu.VMEM)
smem = functools.partial(pl.BlockSpec, memory_space=pltpu.SMEM)
hbm = functools.partial(pl.BlockSpec, memory_space=pl.ANY)


def iota(shape, dim):
    return lax.broadcasted_iota(jnp.int32, shape, dim)


def mxu(a, b, contract):
    return lax.dot_general(a, b, ((contract[:1], contract[1:]), ((), ())), preferred_element_type=f32)


def dispatch_kernel(blocks_dev, me_ref, ids_ref, len_ref, q_ref, place_ref, *send_refs):
    count = len(send_refs)
    slots = send_refs[0].shape[0]
    width = q_ref.shape[1]
    rows, listed = ids_ref.shape
    me = me_ref[0]
    ids = ids_ref[...].astype(f32)
    owner = jnp.floor((ids[:, 0:1] + 0.5) * (1.0 / blocks_dev))
    ahead = owner - me.astype(f32)
    ahead = jnp.where(ahead < 0, ahead + count, ahead)
    lane = iota((rows, lanes), 1)
    hot = jnp.where(lane.astype(f32) == ahead, 1.0, 0.0)
    lower = jnp.where(iota((rows, rows), 1) < iota((rows, rows), 0), 1.0, 0.0)
    before = mxu(lower.astype(bf16), hot.astype(bf16), (1, 0))
    rank = jnp.sum(before * hot, axis=1, keepdims=True)
    target = ahead * slots + rank
    place = jnp.where(iota((rows, count * slots), 1).astype(f32) == target, 1.0, 0.0).astype(bf16)
    place_ref[...] = place
    local = (ids - owner * blocks_dev).astype(bf16)
    eye = jnp.where(iota((listed, lanes), 0) == iota((listed, lanes), 1), 1.0, 0.0).astype(bf16)
    meta = mxu(local, eye, (1, 0))
    spread = jnp.broadcast_to(len_ref[...].astype(f32), (rows, rows))
    length = jnp.sum(
        jnp.where(iota((rows, rows), 0) == iota((rows, rows), 1), spread, 0.0), axis=1, keepdims=True
    )
    high = jnp.floor(length * (1.0 / 64))
    meta = jnp.where(lane == listed, high, meta)
    meta = jnp.where(lane == listed + 1, length - high * 64, meta)
    send = mxu(place, q_ref[...], (0, 0)).astype(bf16)
    send_meta = mxu(place, meta.astype(bf16), (0, 0)).astype(bf16)
    for s in range(count):
        send_refs[s][:, 0:width] = send[s * slots : (s + 1) * slots]
        send_refs[s][:, width : width + lanes] = send_meta[s * slots : (s + 1) * slots]


def dispatch(me, queries, row_blocks, row_len, count, slots, blocks_dev):
    rows, width = queries.shape
    outs = [jax.ShapeDtypeStruct((rows, count * slots), bf16)]
    outs += [jax.ShapeDtypeStruct((slots, width + lanes), bf16)] * count
    got = pl.pallas_call(
        functools.partial(dispatch_kernel, blocks_dev),
        out_shape=outs,
        in_specs=[smem(), vmem(), vmem(), vmem()],
        out_specs=[vmem()] * (count + 1),
        name="dispatch",
    )(me, row_blocks, row_len.reshape(1, rows), queries)
    return got[0], got[1:]


tile_rows = 16


def attend_kernel(count, listed, group, step_blocks, scale_ref, kv_ref, *refs):
    in_refs, out_refs = refs[:count], refs[count : 2 * count]
    kv, qs, os, lens, ints, scalars, kv_sem, int_sem = refs[2 * count :]
    slots = out_refs[0].shape[0]
    width = out_refs[0].shape[1]
    total = count * slots
    places = qs.shape[0]
    heads, tok, dim = kv.shape[2:]
    kv_copy = pltpu.make_async_copy(kv_ref, kv, kv_sem)
    kv_copy.start()

    meta = jnp.concatenate([r[:, width : width + lanes] for r in in_refs], axis=0).astype(f32)
    lane = iota((total, lanes), 1)
    length = jnp.sum(
        jnp.where(lane == listed, meta * 64.0, jnp.where(lane == listed + 1, meta, 0.0)), axis=1, keepdims=True
    )
    ids = jnp.where(lane < listed, meta, 0.0)
    slot = iota((total, 1), 0).astype(f32)
    valid = length > 0.0
    big = float(total)

    def first_list(mask):
        first = jnp.min(jnp.where(mask, slot, big), axis=0, keepdims=True)
        return jnp.sum(jnp.where(slot == first, ids, 0.0), axis=0, keepdims=True)

    list_a = first_list(valid)
    same_a = jnp.sum(jnp.abs(ids - list_a), axis=1, keepdims=True) == 0.0
    in_a = valid & same_a
    in_b = valid & jnp.logical_not(same_a)
    list_b = first_list(in_b)
    span = float(2 * listed * tok)
    key = jnp.where(in_a, 2 * span + length, jnp.where(in_b, span + length, 0.0))
    key = key * total + (total - 1 - slot)
    eye = iota((total, total), 0) == iota((total, total), 1)
    key_row = jnp.sum(jnp.where(eye, key, 0.0), axis=0, keepdims=True)
    len_row = jnp.sum(jnp.where(eye, length, 0.0), axis=0, keepdims=True)
    rank = jnp.sum(jnp.where(key > key_row, 1.0, 0.0), axis=0, keepdims=True)
    a_row = key_row >= 2 * span * total
    b_row = jnp.logical_and(key_row >= span * total, jnp.logical_not(a_row))
    a_count = jnp.sum(jnp.where(a_row, 1.0, 0.0), axis=1, keepdims=True)
    a_tiles = jnp.floor((a_count + (tile_rows - 1)) * (1.0 / tile_rows))
    spot = jnp.where(a_row, rank, jnp.where(b_row, rank - a_count + a_tiles * tile_rows, float(places)))
    placed = iota((places, total), 0).astype(f32) == spot
    perm = jnp.where(placed, 1.0, 0.0).astype(bf16)
    len_sorted = jnp.sum(jnp.where(placed, len_row, 0.0), axis=1, keepdims=True)
    lens[...] = jnp.broadcast_to(len_sorted, (places, lanes)).astype(jnp.int32)
    tops = jnp.sum(
        jnp.where(iota((places, lanes), 0) == iota((places, lanes), 1) * tile_rows, len_sorted, 0.0),
        axis=0,
        keepdims=True,
    )
    row = iota((8, lanes), 0)
    ints[...] = jnp.where(
        row == 0, list_a, jnp.where(row == 1, list_b, jnp.where(row == 2, tops, a_tiles))
    ).astype(jnp.int32)
    int_copy = pltpu.make_async_copy(ints, scalars, int_sem)
    int_copy.start()
    queries = jnp.concatenate([r[:, 0:width] for r in in_refs], axis=0)
    qs[...] = mxu(perm, queries, (1, 0)).astype(bf16)
    os[...] = jnp.zeros_like(os)
    int_copy.wait()
    kv_copy.wait()

    tokens = step_blocks * tok
    tall = group * tile_rows
    factors = [scale_ref[0, k] * (log2_e / math.sqrt(dim)) for k in range(heads)]
    spread = iota((tall, tokens), 1)

    def tile_body(t, _):
        top = scalars[2, t]
        doc = jnp.where(t >= scalars[3, 0], 1, 0)
        at = pl.multiple_of(t * tile_rows, tile_rows)
        spans = jnp.concatenate([lens[pl.ds(at, tile_rows), :]] * group, axis=0)[:, 0:1]
        qt = [
            jnp.concatenate(
                [qs[pl.ds(at, tile_rows), (k * group + g) * dim : (k * group + g + 1) * dim] for g in range(group)],
                axis=0,
            )
            for k in range(heads)
        ]

        def step(c, carry):
            keep = spread < spans - c * tokens
            blocks = [scalars[doc, c * step_blocks + j] for j in range(step_blocks)]
            after = []
            for k in range(heads):
                peak, denom, acc = carry[k]
                keys = jnp.concatenate([kv[b, 0, k] for b in blocks], axis=0)
                scores = mxu(qt[k], keys, (1, 1)) * factors[k]
                scores = jnp.where(keep, scores, -1e30)
                higher = jnp.maximum(peak, jnp.max(scores, axis=1, keepdims=True))
                shrink = jnp.exp2(peak - higher)
                weights = jnp.exp2(scores - higher)
                denom = denom * shrink + jnp.sum(weights, axis=1, keepdims=True)
                values = jnp.concatenate([kv[b, 1, k] for b in blocks], axis=0)
                acc = acc * shrink + mxu(weights.astype(bf16), values, (1, 0))
                after.append((higher, denom, acc))
            return tuple(after)

        start = tuple(
            (jnp.full((tall, 1), -1e30, f32), jnp.zeros((tall, 1), f32), jnp.zeros((tall, dim), f32))
            for _ in range(heads)
        )
        steps = (top + (tokens - 1)) // tokens

        @pl.when(steps > 0)
        def _():
            done = lax.fori_loop(0, steps, step, start)
            for k in range(heads):
                _, denom, acc = done[k]
                out = (acc * (scale_ref[1, k] / denom)).astype(bf16)
                for g in range(group):
                    col = (k * group + g) * dim
                    os[pl.ds(at, tile_rows), col : col + dim] = out[g * tile_rows : (g + 1) * tile_rows]

        return 0

    lax.fori_loop(0, places // tile_rows, tile_body, 0)
    out = mxu(perm, os[...], (0, 0)).astype(bf16)
    for s in range(count):
        out_refs[s][...] = out[s * slots : (s + 1) * slots]


def attend(received, kv_codes, kv_scale, listed, group):
    count = len(received)
    slots, wide = received[0].shape
    width = wide - lanes
    total = count * slots
    places = total + tile_rows
    return pl.pallas_call(
        functools.partial(attend_kernel, count, listed, group, min(8, listed)),
        out_shape=[jax.ShapeDtypeStruct((slots, width), bf16)] * count,
        in_specs=[smem(), hbm()] + [vmem()] * count,
        out_specs=[vmem()] * count,
        scratch_shapes=[
            pltpu.VMEM(kv_codes.shape, bf16),
            pltpu.VMEM((places, width), bf16),
            pltpu.VMEM((places, width), bf16),
            pltpu.VMEM((places, lanes), jnp.int32),
            pltpu.VMEM((8, lanes), jnp.int32),
            pltpu.SMEM((8, lanes), jnp.int32),
            pltpu.SemaphoreType.DMA,
            pltpu.SemaphoreType.DMA,
        ],
        compiler_params=pltpu.CompilerParams(vmem_limit_bytes=32 * mib),
        name="attend",
    )(kv_scale, kv_codes, *received)


def project_kernel(count, parts, at_ref, *refs):
    in_refs, w_ref = refs[:count], refs[count]
    own_ref, out_refs = refs[count + 1], refs[count + 2 : count + 1 + parts]
    x, y = refs[count + 1 + parts :]
    rows = in_refs[0].shape[0]
    piece = own_ref.shape[0]

    @pl.when(pl.program_id(0) == 0)
    def _():
        for s in range(count):
            source = at_ref[0] - s
            source = jnp.where(source < 0, source + count, source)
            x[pl.ds(pl.multiple_of(source * rows, rows), rows), :] = in_refs[s][...]

    y[...] = mxu(x[...], w_ref[...], (1, 0))
    for s in range(parts):
        target = at_ref[1] + s
        target = jnp.where(target >= parts, target - parts, target)
        value = y[pl.ds(pl.multiple_of(target * piece, piece), piece), :]
        if s == 0:
            own_ref[...] = value
        else:
            out_refs[s - 1][...] = value.astype(bf16)


def project(at, pieces, w_out, parts):
    count = len(pieces)
    rows, depth = pieces[0].shape
    cols = w_out.shape[1]
    tall = rows * count
    piece = tall // parts
    wide = 256 if cols % 256 == 0 else cols
    whole = pl.BlockSpec((rows, depth), lambda j: (0, 0))
    part = pl.BlockSpec((piece, wide), lambda j: (0, j))
    got = pl.pallas_call(
        functools.partial(project_kernel, count, parts),
        grid=(cols // wide,),
        out_shape=[jax.ShapeDtypeStruct((piece, cols), f32)]
        + [jax.ShapeDtypeStruct((piece, cols), bf16)] * (parts - 1),
        in_specs=[smem()] + [whole] * count + [pl.BlockSpec((depth, wide), lambda j: (0, j))],
        out_specs=[part] * parts,
        scratch_shapes=[pltpu.VMEM((tall, depth), bf16), pltpu.VMEM((tall, wide), f32)],
        compiler_params=pltpu.CompilerParams(vmem_limit_bytes=32 * mib),
        name="project",
    )(at, *pieces, w_out)
    return got[0], got[1:]


hidden_tile = 256


def swiglu_kernel(row_devs, head_devs, at_ref, gain_ref, *refs):
    pieces = refs[: row_devs * head_devs]
    gate_ref, up_ref, down_ref = refs[row_devs * head_devs : row_devs * head_devs + 3]
    outs = refs[row_devs * head_devs + 3 :]
    keep_refs, send_refs = outs[:row_devs], outs[row_devs : 2 * row_devs]
    x, gate_w, up_w, down_w, inner, y, gate_sem, up_sem, down_sem = outs[2 * row_devs :]
    rows, cols = pieces[0].shape
    tall = x.shape[1]
    hidden = gate_w.shape[1]
    steps = hidden // hidden_tile

    def gate_copy(j):
        cut = pl.ds(j * hidden_tile, hidden_tile)
        return (
            pltpu.make_async_copy(gate_ref.at[:, cut], gate_w.at[:, cut], gate_sem.at[j]),
            pltpu.make_async_copy(up_ref.at[:, cut], up_w.at[:, cut], up_sem.at[j]),
        )

    def down_copy(i):
        cut = pl.ds(i * cols, cols)
        return pltpu.make_async_copy(down_ref.at[:, cut], down_w.at[i], down_sem.at[i])

    for j in range(steps):
        for copy in gate_copy(j):
            copy.start()
    for i in range(row_devs):
        down_copy(i).start()

    me_row, me_head = at_ref[0], at_ref[1]

    def flip(j):
        return me_head + (j & 1) * (1 - 2 * lax.rem(me_head, 2)) + (j & 2) * (1 - lax.rem(lax.div(me_head, 2), 2) * 2)

    def start_of(j):
        return pl.multiple_of(flip(j) * rows, rows)

    def behind(s):
        source = me_row - s
        return jnp.where(source < 0, source + row_devs, source)

    for s in range(row_devs):
        for j in range(head_devs):
            x[behind(s), pl.ds(start_of(j), rows), :] = pieces[s * head_devs + j][...]
    squares = jnp.zeros((tall, 1), f32)
    for z in range(row_devs):
        value = x[z].astype(f32)
        squares = squares + jnp.sum(value * value, axis=1, keepdims=True)
    inverse = lax.rsqrt(squares / (row_devs * cols) + norm_eps)
    for z in range(row_devs):
        x[z] = (x[z].astype(f32) * inverse * gain_ref[:, z * cols : (z + 1) * cols]).astype(bf16)

    for j in range(steps):
        for copy in gate_copy(j):
            copy.wait()
        cut = slice(j * hidden_tile, (j + 1) * hidden_tile)
        gate = jnp.zeros((tall, hidden_tile), f32)
        up = jnp.zeros((tall, hidden_tile), f32)
        for z in range(row_devs):
            gate = gate + mxu(x[z], gate_w[z * cols : (z + 1) * cols, cut], (1, 0))
            up = up + mxu(x[z], up_w[z * cols : (z + 1) * cols, cut], (1, 0))
        inner[:, cut] = (gate / (1.0 + jnp.exp(-gate)) * up).astype(bf16)

    for i in range(row_devs):
        down_copy(i).wait()

        @pl.loop(0, cols // hidden_tile)
        def _(t):
            cut = pl.ds(pl.multiple_of(t * hidden_tile, hidden_tile), hidden_tile)
            y[i, :, cut] = mxu(inner[...], down_w[i, :, cut], (1, 0))

    for i in range(row_devs):
        target = me_row + i
        target = jnp.where(target >= row_devs, target - row_devs, target)
        for j in range(head_devs):
            value = y[target, pl.ds(start_of(j), rows), :]
            half = slice((j // 2) * rows, (j // 2 + 1) * rows)
            if j % 2 == 0:
                keep_refs[i][half, :] = value
            else:
                send_refs[i][half, :] = value.astype(bf16)


def swiglu(at, pieces, gain, w_gate, w_up, w_down, row_devs, head_devs):
    rows, cols = pieces[0].shape
    tall = rows * head_devs
    width, hidden = w_gate.shape
    half = rows * head_devs // 2
    steps = hidden // hidden_tile
    got = pl.pallas_call(
        functools.partial(swiglu_kernel, row_devs, head_devs),
        out_shape=[jax.ShapeDtypeStruct((half, cols), f32)] * row_devs
        + [jax.ShapeDtypeStruct((half, cols), bf16)] * row_devs,
        in_specs=[smem(), vmem()] + [vmem()] * len(pieces) + [hbm()] * 3,
        out_specs=[vmem()] * (2 * row_devs),
        scratch_shapes=[
            pltpu.VMEM((row_devs, tall, cols), bf16),
            pltpu.VMEM((width, hidden), bf16),
            pltpu.VMEM((width, hidden), bf16),
            pltpu.VMEM((row_devs, hidden, cols), bf16),
            pltpu.VMEM((tall, hidden), bf16),
            pltpu.VMEM((row_devs, tall, cols), f32),
            pltpu.SemaphoreType.DMA((steps,)),
            pltpu.SemaphoreType.DMA((steps,)),
            pltpu.SemaphoreType.DMA((row_devs,)),
        ],
        compiler_params=pltpu.CompilerParams(vmem_limit_bytes=52 * mib),
        name="swiglu",
    )(at, gain.reshape(1, width), *pieces, w_gate, w_up, w_down)
    return got[:row_devs], got[row_devs:]


def shift(x, axis, step):
    n = lax.axis_size(axis)
    return lax.ppermute(x, axis, [(i, (i + step) % n) for i in range(n)])


def swap(x, axis, flip):
    return lax.ppermute(x, axis, [(i, i ^ flip) for i in range(lax.axis_size(axis))])


def feed_forward(at, hidden_state, norm_gain, w_gate, w_up, w_down):
    row_devs = lax.axis_size("rows")
    head_devs = lax.axis_size("heads")
    rows = hidden_state.shape[0]
    pieces = []
    for s in range(row_devs):
        piece = shift(hidden_state, "rows", s) if s else hidden_state
        across = swap(piece, "heads", 2)
        pieces += [piece, swap(piece, "heads", 1), across, swap(across, "heads", 1)]
    keeps, sends = swiglu(at, pieces, norm_gain, w_gate, w_up, w_down, row_devs, head_devs)
    total = hidden_state.astype(f32)
    order = sorted(range(row_devs), key=lambda i: (i == 0, abs(2 * i - row_devs)))
    for i in order:
        pair = keeps[i] + swap(sends[i], "heads", 1).astype(f32)
        part = pair[:rows] + swap(pair[rows:].astype(bf16), "heads", 2).astype(f32)
        total = total + (shift(part.astype(bf16), "rows", i).astype(f32) if i else part)
    return total.astype(bf16)


def feed_forward_gathered(hidden_state, norm_gain, w_gate, w_up, w_down):
    model_width = norm_gain.shape[0]
    full_rows = lax.all_gather(hidden_state, "rows", axis=1, tiled=True)
    every = lax.all_gather(full_rows, "heads", axis=0, tiled=True).astype(f32)
    totals = jnp.sum(every * every, axis=1)
    normed = (every * lax.rsqrt(totals / model_width + norm_eps)[:, None] * norm_gain).astype(bf16)
    gate = jnp.dot(normed, w_gate, preferred_element_type=f32)
    up = jnp.dot(normed, w_up, preferred_element_type=f32)
    inner = (jax.nn.silu(gate) * up).astype(bf16)
    partial_sum = jnp.dot(inner, w_down, preferred_element_type=f32).astype(bf16)
    section = lax.psum_scatter(partial_sum, "heads", scatter_dimension=0, tiled=True)
    ffn = lax.psum_scatter(section, "rows", scatter_dimension=1, tiled=True)
    return (hidden_state.astype(f32) + ffn.astype(f32)).astype(bf16)


def shards(
    resid, queries, kv_codes, kv_scale, row_blocks, row_len, w_out, norm_gain, w_gate, w_up, w_down
):
    row_devs = lax.axis_size("rows")
    head_devs = lax.axis_size("heads")
    rows_dev, width_q = queries.shape
    listed = row_blocks.shape[1]
    blocks_dev = kv_codes.shape[0]
    heads_dev, head_dim = kv_codes.shape[2], kv_codes.shape[4]
    group = width_q // (heads_dev * head_dim)
    capacity = max(2, 2 * rows_dev // row_devs)
    slots = -(-capacity // 16) * 16
    my_row = lax.axis_index("rows").astype(jnp.int32)
    my_head = lax.axis_index("heads").astype(jnp.int32)
    at = jnp.stack([my_row, my_head])

    place, sends = dispatch(at, queries, row_blocks, row_len, row_devs, slots, blocks_dev)
    received = [sends[0]] + [shift(sends[s], "rows", s) for s in range(1, row_devs)]
    results = attend(received, kv_codes, kv_scale, listed, group)
    back = [results[0]] + [shift(results[s], "rows", -s) for s in range(1, row_devs)]
    attended = jnp.dot(place, jnp.concatenate(back, axis=0), preferred_element_type=f32).astype(bf16)
    pieces = [attended] + [shift(attended, "rows", s) for s in range(1, row_devs)]
    own, others = project(at, pieces, w_out, head_devs)
    attn_out = own
    for s in range(1, head_devs):
        attn_out = attn_out + shift(others[s - 1], "heads", s).astype(f32)
    hidden_state = (resid.astype(f32) + attn_out).astype(bf16)

    if head_devs == 4 and hidden_state.shape[1] % hidden_tile == 0:
        return feed_forward(at, hidden_state, norm_gain, w_gate, w_up, w_down)
    return feed_forward_gathered(hidden_state, norm_gain, w_gate, w_up, w_down)


def solution(mesh):
    placed = (
        P(("groups", "heads"), "rows"),
        P(("groups", "rows"), "heads"),
        P(("groups", "rows"), None, "heads", None, None),
        P("groups", "heads"),
        P(("groups", "rows"), None),
        P(("groups", "rows")),
        P("heads", "rows"),
        P(),
        P(None, ("rows", "heads")),
        P(None, ("rows", "heads")),
        P(("rows", "heads"), None),
    )
    return jax.shard_map(
        shards,
        mesh=mesh,
        in_specs=placed,
        out_specs=P(("groups", "heads"), "rows"),
        check_vma=False,
    )
```

```python
import functools
import math

import jax
import jax.numpy as jnp
from jax import lax
from jax.experimental import pallas as pl
from jax.experimental.pallas import tpu as pltpu
from jax.sharding import PartitionSpec as P

norm_eps = 1e-06
log2_e = 1.4426950408889634
mib = 1 << 20
lanes = 128
f32 = jnp.float32
bf16 = jnp.bfloat16

vmem = functools.partial(pl.BlockSpec, memory_space=pltpu.VMEM)
smem = functools.partial(pl.BlockSpec, memory_space=pltpu.SMEM)
hbm = functools.partial(pl.BlockSpec, memory_space=pltpu.HBM)


def stay(x):
    return pltpu.with_memory_space_constraint(x, pltpu.HBM)


def iota(shape, dim):
    return lax.broadcasted_iota(jnp.int32, shape, dim)


def mxu(a, b, contract):
    return lax.dot_general(a, b, ((contract[:1], contract[1:]), ((), ())), preferred_element_type=f32)


def fetch_kernel(count, after_ref, *refs):
    sources, targets, sems = refs[:count], refs[count : 2 * count], refs[2 * count]
    copies = [pltpu.make_async_copy(sources[i], targets[i], sems.at[i]) for i in range(count)]
    for copy in copies:
        copy.start()
    for copy in copies:
        copy.wait()


def fetch(after, *arrays):
    count = len(arrays)
    return pl.pallas_call(
        functools.partial(fetch_kernel, count),
        out_shape=[pltpu.VMEM(a.shape, a.dtype) for a in arrays],
        in_specs=[pl.BlockSpec(memory_space=pl.ANY)] + [hbm()] * count,
        out_specs=[vmem()] * count,
        scratch_shapes=[pltpu.SemaphoreType.DMA((count,))],
        cost_estimate=pl.CostEstimate(
            flops=0, bytes_accessed=sum(a.size * a.dtype.itemsize for a in arrays), transcendentals=0
        ),
        compiler_params=pltpu.CompilerParams(vmem_limit_bytes=1 * mib),
        name="fetch",
    )(after, *map(stay, arrays))


def dispatch_kernel(blocks_dev, me_ref, ids_ref, len_ref, q_ref, place_ref, *send_refs):
    count = len(send_refs)
    slots = send_refs[0].shape[0]
    width = q_ref.shape[1]
    rows, listed = ids_ref.shape
    me = me_ref[0]
    ids = ids_ref[...].astype(f32)
    owner = jnp.floor((ids[:, 0:1] + 0.5) * (1.0 / blocks_dev))
    ahead = owner - me.astype(f32)
    ahead = jnp.where(ahead < 0, ahead + count, ahead)
    lane = iota((rows, lanes), 1)
    hot = jnp.where(lane.astype(f32) == ahead, 1.0, 0.0)
    lower = jnp.where(iota((rows, rows), 1) < iota((rows, rows), 0), 1.0, 0.0)
    before = mxu(lower.astype(bf16), hot.astype(bf16), (1, 0))
    rank = jnp.sum(before * hot, axis=1, keepdims=True)
    target = ahead * slots + rank
    place = jnp.where(iota((rows, count * slots), 1).astype(f32) == target, 1.0, 0.0).astype(bf16)
    place_ref[...] = place
    local = (ids - owner * blocks_dev).astype(bf16)
    eye = jnp.where(iota((listed, lanes), 0) == iota((listed, lanes), 1), 1.0, 0.0).astype(bf16)
    meta = mxu(local, eye, (1, 0))
    spread = jnp.broadcast_to(len_ref[...].astype(f32), (rows, rows))
    length = jnp.sum(
        jnp.where(iota((rows, rows), 0) == iota((rows, rows), 1), spread, 0.0), axis=1, keepdims=True
    )
    high = jnp.floor(length * (1.0 / 64))
    meta = jnp.where(lane == listed, high, meta)
    meta = jnp.where(lane == listed + 1, length - high * 64, meta)
    send = mxu(place, q_ref[...], (0, 0)).astype(bf16)
    send_meta = mxu(place, meta.astype(bf16), (0, 0)).astype(bf16)
    for s in range(count):
        send_refs[s][:, 0:width] = send[s * slots : (s + 1) * slots]
        send_refs[s][:, width : width + lanes] = send_meta[s * slots : (s + 1) * slots]


def dispatch(me, queries, row_blocks, row_len, count, slots, blocks_dev):
    rows, width = queries.shape
    outs = [jax.ShapeDtypeStruct((rows, count * slots), bf16)]
    outs += [jax.ShapeDtypeStruct((slots, width + lanes), bf16)] * count
    got = pl.pallas_call(
        functools.partial(dispatch_kernel, blocks_dev),
        out_shape=outs,
        in_specs=[smem(), vmem(), vmem(), vmem()],
        out_specs=[vmem()] * (count + 1),
        compiler_params=pltpu.CompilerParams(vmem_limit_bytes=8 * mib),
        name="dispatch",
    )(me, row_blocks, row_len.reshape(1, rows), queries)
    return got[0], got[1:]


tile_rows = 16


def attend_kernel(count, later, listed, group, step_blocks, scale_ref, kv, *refs):
    in_refs, refs = refs[:count], refs[count:]
    later_refs, refs = refs[:later], refs[later:]
    out_refs, refs = refs[:count], refs[count:]
    later_outs, refs = refs[:later], refs[later:]
    qs, os, lens, ints, scalars, later_sems, int_sem = refs
    copies = [pltpu.make_async_copy(later_refs[i], later_outs[i], later_sems.at[i]) for i in range(later)]
    for copy in copies:
        copy.start()
    slots = out_refs[0].shape[0]
    width = out_refs[0].shape[1]
    total = count * slots
    places = qs.shape[0]
    heads, tok, dim = kv.shape[2:]
    meta = jnp.concatenate([r[:, width : width + lanes] for r in in_refs], axis=0).astype(f32)
    lane = iota((total, lanes), 1)
    length = jnp.sum(
        jnp.where(lane == listed, meta * 64.0, jnp.where(lane == listed + 1, meta, 0.0)), axis=1, keepdims=True
    )
    ids = jnp.where(lane < listed, meta, 0.0)
    slot = iota((total, 1), 0).astype(f32)
    valid = length > 0.0
    big = float(total)

    def first_list(mask):
        first = jnp.min(jnp.where(mask, slot, big), axis=0, keepdims=True)
        return jnp.sum(jnp.where(slot == first, ids, 0.0), axis=0, keepdims=True)

    list_a = first_list(valid)
    same_a = jnp.sum(jnp.abs(ids - list_a), axis=1, keepdims=True) == 0.0
    in_a = valid & same_a
    in_b = valid & jnp.logical_not(same_a)
    list_b = first_list(in_b)
    span = float(2 * listed * tok)
    key = jnp.where(in_a, 2 * span + length, jnp.where(in_b, span + length, 0.0))
    key = key * total + (total - 1 - slot)
    eye = iota((total, total), 0) == iota((total, total), 1)
    key_row = jnp.sum(jnp.where(eye, key, 0.0), axis=0, keepdims=True)
    len_row = jnp.sum(jnp.where(eye, length, 0.0), axis=0, keepdims=True)
    rank = jnp.sum(jnp.where(key > key_row, 1.0, 0.0), axis=0, keepdims=True)
    a_row = key_row >= 2 * span * total
    b_row = jnp.logical_and(key_row >= span * total, jnp.logical_not(a_row))
    a_count = jnp.sum(jnp.where(a_row, 1.0, 0.0), axis=1, keepdims=True)
    a_tiles = jnp.floor((a_count + (tile_rows - 1)) * (1.0 / tile_rows))
    spot = jnp.where(a_row, rank, jnp.where(b_row, rank - a_count + a_tiles * tile_rows, float(places)))
    placed = iota((places, total), 0).astype(f32) == spot
    perm = jnp.where(placed, 1.0, 0.0).astype(bf16)
    len_sorted = jnp.sum(jnp.where(placed, len_row, 0.0), axis=1, keepdims=True)
    lens[...] = jnp.broadcast_to(len_sorted, (places, lanes)).astype(jnp.int32)
    tops = jnp.sum(
        jnp.where(iota((places, lanes), 0) == iota((places, lanes), 1) * tile_rows, len_sorted, 0.0),
        axis=0,
        keepdims=True,
    )
    row = iota((8, lanes), 0)
    ints[...] = jnp.where(
        row == 0, list_a, jnp.where(row == 1, list_b, jnp.where(row == 2, tops, a_tiles))
    ).astype(jnp.int32)
    int_copy = pltpu.make_async_copy(ints, scalars, int_sem)
    int_copy.start()
    queries = jnp.concatenate([r[:, 0:width] for r in in_refs], axis=0)
    qs[...] = mxu(perm, queries, (1, 0)).astype(bf16)
    os[...] = jnp.zeros_like(os)
    int_copy.wait()

    tokens = step_blocks * tok
    tall = group * tile_rows
    factors = [scale_ref[0, k] * (log2_e / math.sqrt(dim)) for k in range(heads)]
    spread = iota((tall, tokens), 1)

    def tile_body(t, _):
        top = scalars[2, t]
        doc = jnp.where(t >= scalars[3, 0], 1, 0)
        at = pl.multiple_of(t * tile_rows, tile_rows)
        spans = jnp.concatenate([lens[pl.ds(at, tile_rows), :]] * group, axis=0)[:, 0:1]
        qt = [
            jnp.concatenate(
                [qs[pl.ds(at, tile_rows), (k * group + g) * dim : (k * group + g + 1) * dim] for g in range(group)],
                axis=0,
            )
            for k in range(heads)
        ]

        def step(c, carry):
            keep = spread < spans - c * tokens
            blocks = [scalars[doc, c * step_blocks + j] for j in range(step_blocks)]
            after = []
            for k in range(heads):
                peak, denom, acc = carry[k]
                keys = jnp.concatenate([kv[b, 0, k] for b in blocks], axis=0)
                scores = mxu(qt[k], keys, (1, 1)) * factors[k]
                scores = jnp.where(keep, scores, -1e30)
                higher = jnp.maximum(peak, jnp.max(scores, axis=1, keepdims=True))
                shrink = jnp.exp2(peak - higher)
                weights = jnp.exp2(scores - higher)
                denom = denom * shrink + jnp.sum(weights, axis=1, keepdims=True)
                values = jnp.concatenate([kv[b, 1, k] for b in blocks], axis=0)
                acc = acc * shrink + mxu(weights.astype(bf16), values, (1, 0))
                after.append((higher, denom, acc))
            return tuple(after)

        start = tuple(
            (jnp.full((tall, 1), -1e30, f32), jnp.zeros((tall, 1), f32), jnp.zeros((tall, dim), f32))
            for _ in range(heads)
        )
        steps = (top + (tokens - 1)) // tokens

        @pl.when(steps > 0)
        def _():
            done = lax.fori_loop(0, steps, step, start)
            for k in range(heads):
                _, denom, acc = done[k]
                out = (acc * (scale_ref[1, k] / denom)).astype(bf16)
                for g in range(group):
                    col = (k * group + g) * dim
                    os[pl.ds(at, tile_rows), col : col + dim] = out[g * tile_rows : (g + 1) * tile_rows]

        return 0

    lax.fori_loop(0, places // tile_rows, tile_body, 0)
    out = mxu(perm, os[...], (0, 0)).astype(bf16)
    for s in range(count):
        out_refs[s][...] = out[s * slots : (s + 1) * slots]
    for copy in copies:
        copy.wait()


def attend(received, kv_codes, kv_scale, later, listed, group):
    count = len(received)
    slots, wide = received[0].shape
    width = wide - lanes
    total = count * slots
    places = total + tile_rows
    got = pl.pallas_call(
        functools.partial(attend_kernel, count, len(later), listed, group, min(8, listed)),
        out_shape=[jax.ShapeDtypeStruct((slots, width), bf16)] * count
        + [pltpu.VMEM(a.shape, a.dtype) for a in later],
        in_specs=[smem()] + [vmem()] * (count + 1) + [hbm()] * len(later),
        out_specs=[vmem()] * (count + len(later)),
        scratch_shapes=[
            pltpu.VMEM((places, width), bf16),
            pltpu.VMEM((places, width), bf16),
            pltpu.VMEM((places, lanes), jnp.int32),
            pltpu.VMEM((8, lanes), jnp.int32),
            pltpu.SMEM((8, lanes), jnp.int32),
            pltpu.SemaphoreType.DMA((max(1, len(later)),)),
            pltpu.SemaphoreType.DMA,
        ],
        compiler_params=pltpu.CompilerParams(vmem_limit_bytes=12 * mib),
        name="attend",
    )(kv_scale, kv_codes, *received, *map(stay, later))
    return got[:count], got[count:]


def project_kernel(count, parts, at_ref, *refs):
    in_refs, w_ref = refs[:count], refs[count]
    own_ref, out_refs = refs[count + 1], refs[count + 2 : count + 1 + parts]
    x, y = refs[count + 1 + parts :]
    rows = in_refs[0].shape[0]
    piece = own_ref.shape[0]

    @pl.when(pl.program_id(0) == 0)
    def _():
        for s in range(count):
            source = at_ref[0] - s
            source = jnp.where(source < 0, source + count, source)
            x[pl.ds(pl.multiple_of(source * rows, rows), rows), :] = in_refs[s][...]

    y[...] = mxu(x[...], w_ref[...], (1, 0))
    for s in range(parts):
        target = at_ref[1] + s
        target = jnp.where(target >= parts, target - parts, target)
        value = y[pl.ds(pl.multiple_of(target * piece, piece), piece), :]
        if s == 0:
            own_ref[...] = value
        else:
            out_refs[s - 1][...] = value.astype(bf16)


def project(at, pieces, w_out, parts):
    count = len(pieces)
    rows, depth = pieces[0].shape
    cols = w_out.shape[1]
    tall = rows * count
    piece = tall // parts
    wide = 256 if cols % 256 == 0 else cols
    whole = pl.BlockSpec((rows, depth), lambda j: (0, 0))
    part = pl.BlockSpec((piece, wide), lambda j: (0, j))
    got = pl.pallas_call(
        functools.partial(project_kernel, count, parts),
        grid=(cols // wide,),
        out_shape=[jax.ShapeDtypeStruct((piece, cols), f32)]
        + [jax.ShapeDtypeStruct((piece, cols), bf16)] * (parts - 1),
        in_specs=[smem()] + [whole] * count + [pl.BlockSpec((depth, wide), lambda j: (0, j))],
        out_specs=[part] * parts,
        scratch_shapes=[pltpu.VMEM((tall, depth), bf16), pltpu.VMEM((tall, wide), f32)],
        compiler_params=pltpu.CompilerParams(vmem_limit_bytes=12 * mib),
        name="project",
    )(at, *pieces, w_out)
    return got[0], got[1:]


hidden_tile = 256


def swiglu_kernel(row_devs, head_devs, at_ref, gain_ref, *refs):
    pieces = refs[: row_devs * head_devs]
    gate_ref, up_ref, down_ref = refs[row_devs * head_devs : row_devs * head_devs + 3]
    outs = refs[row_devs * head_devs + 3 :]
    keep_refs, send_refs = outs[:row_devs], outs[row_devs : 2 * row_devs]
    x, inner, y = outs[2 * row_devs :]
    rows, cols = pieces[0].shape
    tall = x.shape[1]
    hidden = gate_ref.shape[1]
    steps = hidden // hidden_tile

    me_row, me_head = at_ref[0], at_ref[1]

    def flip(j):
        return me_head + (j & 1) * (1 - 2 * lax.rem(me_head, 2)) + (j & 2) * (1 - lax.rem(lax.div(me_head, 2), 2) * 2)

    def start_of(j):
        return pl.multiple_of(flip(j) * rows, rows)

    def behind(s):
        source = me_row - s
        return jnp.where(source < 0, source + row_devs, source)

    for s in range(row_devs):
        for j in range(head_devs):
            x[behind(s), pl.ds(start_of(j), rows), :] = pieces[s * head_devs + j][...]
    squares = jnp.zeros((tall, 1), f32)
    for z in range(row_devs):
        value = x[z].astype(f32)
        squares = squares + jnp.sum(value * value, axis=1, keepdims=True)
    inverse = lax.rsqrt(squares / (row_devs * cols) + norm_eps)
    for z in range(row_devs):
        x[z] = (x[z].astype(f32) * inverse * gain_ref[:, z * cols : (z + 1) * cols]).astype(bf16)

    for j in range(steps):
        cut = slice(j * hidden_tile, (j + 1) * hidden_tile)
        gate = jnp.zeros((tall, hidden_tile), f32)
        up = jnp.zeros((tall, hidden_tile), f32)
        for z in range(row_devs):
            gate = gate + mxu(x[z], gate_ref[z * cols : (z + 1) * cols, cut], (1, 0))
            up = up + mxu(x[z], up_ref[z * cols : (z + 1) * cols, cut], (1, 0))
        inner[:, cut] = (gate / (1.0 + jnp.exp(-gate)) * up).astype(bf16)

    for i in range(row_devs):
        @pl.loop(0, cols // hidden_tile)
        def _(t):
            cut = pl.ds(pl.multiple_of(t * hidden_tile, hidden_tile), hidden_tile)
            from_cut = pl.ds(pl.multiple_of(i * cols + t * hidden_tile, hidden_tile), hidden_tile)
            y[i, :, cut] = mxu(inner[...], down_ref[:, from_cut], (1, 0))

    for i in range(row_devs):
        target = me_row + i
        target = jnp.where(target >= row_devs, target - row_devs, target)
        for j in range(head_devs):
            value = y[target, pl.ds(start_of(j), rows), :]
            half = slice((j // 2) * rows, (j // 2 + 1) * rows)
            if j % 2 == 0:
                keep_refs[i][half, :] = value
            else:
                send_refs[i][half, :] = value.astype(bf16)


def swiglu(at, pieces, gain, w_gate, w_up, w_down, row_devs, head_devs):
    rows, cols = pieces[0].shape
    tall = rows * head_devs
    width, hidden = w_gate.shape
    half = rows * head_devs // 2
    got = pl.pallas_call(
        functools.partial(swiglu_kernel, row_devs, head_devs),
        out_shape=[jax.ShapeDtypeStruct((half, cols), f32)] * row_devs
        + [jax.ShapeDtypeStruct((half, cols), bf16)] * row_devs,
        in_specs=[smem(), vmem()] + [vmem()] * (len(pieces) + 3),
        out_specs=[vmem()] * (2 * row_devs),
        scratch_shapes=[
            pltpu.VMEM((row_devs, tall, cols), bf16),
            pltpu.VMEM((tall, hidden), bf16),
            pltpu.VMEM((row_devs, tall, cols), f32),
        ],
        compiler_params=pltpu.CompilerParams(vmem_limit_bytes=12 * mib),
        name="swiglu",
    )(at, gain.reshape(1, width), *pieces, w_gate, w_up, w_down)
    return got[:row_devs], got[row_devs:]


def shift(x, axis, step):
    n = lax.axis_size(axis)
    return lax.ppermute(x, axis, [(i, (i + step) % n) for i in range(n)])


def swap(x, axis, flip):
    return lax.ppermute(x, axis, [(i, i ^ flip) for i in range(lax.axis_size(axis))])


def feed_forward(at, hidden_state, norm_gain, w_gate, w_up, w_down):
    row_devs = lax.axis_size("rows")
    head_devs = lax.axis_size("heads")
    rows = hidden_state.shape[0]
    pieces = []
    for s in range(row_devs):
        piece = shift(hidden_state, "rows", s) if s else hidden_state
        across = swap(piece, "heads", 2)
        pieces += [piece, swap(piece, "heads", 1), across, swap(across, "heads", 1)]
    keeps, sends = swiglu(at, pieces, norm_gain, w_gate, w_up, w_down, row_devs, head_devs)
    total = hidden_state.astype(f32)
    order = sorted(range(row_devs), key=lambda i: (i == 0, abs(2 * i - row_devs)))
    for i in order:
        pair = keeps[i] + swap(sends[i], "heads", 1).astype(f32)
        part = pair[:rows] + swap(pair[rows:].astype(bf16), "heads", 2).astype(f32)
        total = total + (shift(part.astype(bf16), "rows", i).astype(f32) if i else part)
    return total.astype(bf16)


def feed_forward_gathered(hidden_state, norm_gain, w_gate, w_up, w_down):
    model_width = norm_gain.shape[0]
    full_rows = lax.all_gather(hidden_state, "rows", axis=1, tiled=True)
    every = lax.all_gather(full_rows, "heads", axis=0, tiled=True).astype(f32)
    totals = jnp.sum(every * every, axis=1)
    normed = (every * lax.rsqrt(totals / model_width + norm_eps)[:, None] * norm_gain).astype(bf16)
    gate = jnp.dot(normed, w_gate, preferred_element_type=f32)
    up = jnp.dot(normed, w_up, preferred_element_type=f32)
    inner = (jax.nn.silu(gate) * up).astype(bf16)
    partial_sum = jnp.dot(inner, w_down, preferred_element_type=f32).astype(bf16)
    section = lax.psum_scatter(partial_sum, "heads", scatter_dimension=0, tiled=True)
    ffn = lax.psum_scatter(section, "rows", scatter_dimension=1, tiled=True)
    return (hidden_state.astype(f32) + ffn.astype(f32)).astype(bf16)


def shards(
    resid, queries, kv_codes, kv_scale, row_blocks, row_len, w_out, norm_gain, w_gate, w_up, w_down
):
    row_devs = lax.axis_size("rows")
    head_devs = lax.axis_size("heads")
    rows_dev, width_q = queries.shape
    listed = row_blocks.shape[1]
    blocks_dev = kv_codes.shape[0]
    heads_dev, head_dim = kv_codes.shape[2], kv_codes.shape[4]
    group = width_q // (heads_dev * head_dim)
    capacity = max(2, 2 * rows_dev // row_devs)
    slots = -(-capacity // 16) * 16
    my_row = lax.axis_index("rows").astype(jnp.int32)
    my_head = lax.axis_index("heads").astype(jnp.int32)
    at = jnp.stack([my_row, my_head])

    place, sends = dispatch(at, queries, row_blocks, row_len, row_devs, slots, blocks_dev)
    received = [sends[0]] + [shift(sends[s], "rows", s) for s in range(1, row_devs)]
    (kv_near,) = fetch(place, kv_codes)
    results, (w_gate, w_out) = attend(received, kv_near, kv_scale, (w_gate, w_out), listed, group)
    back = [results[0]] + [shift(results[s], "rows", -s) for s in range(1, row_devs)]
    attended = jnp.dot(place, jnp.concatenate(back, axis=0), preferred_element_type=f32).astype(bf16)
    pieces = [attended] + [shift(attended, "rows", s) for s in range(1, row_devs)]
    pieces, w_up, w_down = lax.optimization_barrier((pieces, *fetch(attended, w_up, w_down)))
    own, others = project(at, pieces, w_out, head_devs)
    attn_out = own
    for s in range(1, head_devs):
        attn_out = attn_out + shift(others[s - 1], "heads", s).astype(f32)
    hidden_state = (resid.astype(f32) + attn_out).astype(bf16)

    if head_devs == 4 and hidden_state.shape[1] % hidden_tile == 0:
        return feed_forward(at, hidden_state, norm_gain, w_gate, w_up, w_down)
    return feed_forward_gathered(hidden_state, norm_gain, w_gate, w_up, w_down)


def solution(mesh):
    placed = (
        P(("groups", "heads"), "rows"),
        P(("groups", "rows"), "heads"),
        P(("groups", "rows"), None, "heads", None, None),
        P("groups", "heads"),
        P(("groups", "rows"), None),
        P(("groups", "rows")),
        P("heads", "rows"),
        P(),
        P(None, ("rows", "heads")),
        P(None, ("rows", "heads")),
        P(("rows", "heads"), None),
    )
    return jax.shard_map(
        shards,
        mesh=mesh,
        in_specs=placed,
        out_specs=P(("groups", "heads"), "rows"),
        check_vma=False,
    )
```

```python
import functools
import math

import jax
import jax.numpy as jnp
from jax import lax
from jax.experimental import pallas as pl
from jax.experimental.pallas import tpu as pltpu
from jax.sharding import PartitionSpec as P

norm_eps = 1e-06
log2_e = 1.4426950408889634
mib = 1 << 20
lanes = 128
f32 = jnp.float32
bf16 = jnp.bfloat16

vmem = functools.partial(pl.BlockSpec, memory_space=pltpu.VMEM)
smem = functools.partial(pl.BlockSpec, memory_space=pltpu.SMEM)
hbm = functools.partial(pl.BlockSpec, memory_space=pltpu.HBM)


def stay(x):
    return pltpu.with_memory_space_constraint(x, pltpu.HBM)


def iota(shape, dim):
    return lax.broadcasted_iota(jnp.int32, shape, dim)


def mxu(a, b, contract):
    return lax.dot_general(a, b, ((contract[:1], contract[1:]), ((), ())), preferred_element_type=f32)


def fetch_kernel(count, after_ref, *refs):
    sources, targets, sems = refs[:count], refs[count : 2 * count], refs[2 * count]
    copies = [pltpu.make_async_copy(sources[i], targets[i], sems.at[i]) for i in range(count)]
    for copy in copies:
        copy.start()
    for copy in copies:
        copy.wait()


def fetch(after, *arrays):
    count = len(arrays)
    return pl.pallas_call(
        functools.partial(fetch_kernel, count),
        out_shape=[pltpu.VMEM(a.shape, a.dtype) for a in arrays],
        in_specs=[pl.BlockSpec(memory_space=pl.ANY)] + [hbm()] * count,
        out_specs=[vmem()] * count,
        scratch_shapes=[pltpu.SemaphoreType.DMA((count,))],
        cost_estimate=pl.CostEstimate(
            flops=0, bytes_accessed=sum(a.size * a.dtype.itemsize for a in arrays), transcendentals=0
        ),
        compiler_params=pltpu.CompilerParams(vmem_limit_bytes=1 * mib),
        name="fetch",
    )(after, *map(stay, arrays))


def dispatch_kernel(blocks_dev, me_ref, ids_hbm, len_hbm, q_hbm, place_ref, *refs):
    send_refs, (ids_ref, len_ref, q_ref, sems) = refs[:-4], refs[-4:]
    ids_copy = pltpu.make_async_copy(ids_hbm, ids_ref, sems.at[0])
    len_copy = pltpu.make_async_copy(len_hbm, len_ref, sems.at[1])
    q_copy = pltpu.make_async_copy(q_hbm, q_ref, sems.at[2])
    for copy in (ids_copy, len_copy, q_copy):
        copy.start()
    count = len(send_refs)
    slots = send_refs[0].shape[0]
    width = q_ref.shape[1]
    rows, listed = ids_ref.shape
    me = me_ref[0]
    ids_copy.wait()
    len_copy.wait()
    ids = ids_ref[...].astype(f32)
    owner = jnp.floor((ids[:, 0:1] + 0.5) * (1.0 / blocks_dev))
    ahead = owner - me.astype(f32)
    ahead = jnp.where(ahead < 0, ahead + count, ahead)
    lane = iota((rows, lanes), 1)
    hot = jnp.where(lane.astype(f32) == ahead, 1.0, 0.0)
    lower = jnp.where(iota((rows, rows), 1) < iota((rows, rows), 0), 1.0, 0.0)
    before = mxu(lower.astype(bf16), hot.astype(bf16), (1, 0))
    rank = jnp.sum(before * hot, axis=1, keepdims=True)
    target = ahead * slots + rank
    place = jnp.where(iota((rows, count * slots), 1).astype(f32) == target, 1.0, 0.0).astype(bf16)
    place_ref[...] = place
    local = (ids - owner * blocks_dev).astype(bf16)
    eye = jnp.where(iota((listed, lanes), 0) == iota((listed, lanes), 1), 1.0, 0.0).astype(bf16)
    meta = mxu(local, eye, (1, 0))
    spread = jnp.broadcast_to(len_ref[...].astype(f32), (rows, rows))
    length = jnp.sum(
        jnp.where(iota((rows, rows), 0) == iota((rows, rows), 1), spread, 0.0), axis=1, keepdims=True
    )
    high = jnp.floor(length * (1.0 / 64))
    meta = jnp.where(lane == listed, high, meta)
    meta = jnp.where(lane == listed + 1, length - high * 64, meta)
    q_copy.wait()
    send = mxu(place, q_ref[...], (0, 0)).astype(bf16)
    send_meta = mxu(place, meta.astype(bf16), (0, 0)).astype(bf16)
    for s in range(count):
        send_refs[s][:, 0:width] = send[s * slots : (s + 1) * slots]
        send_refs[s][:, width : width + lanes] = send_meta[s * slots : (s + 1) * slots]


def dispatch(me, queries, row_blocks, row_len, count, slots, blocks_dev):
    rows, width = queries.shape
    outs = [jax.ShapeDtypeStruct((rows, count * slots), bf16)]
    outs += [jax.ShapeDtypeStruct((slots, width + lanes), bf16)] * count
    got = pl.pallas_call(
        functools.partial(dispatch_kernel, blocks_dev),
        out_shape=outs,
        in_specs=[smem(), hbm(), hbm(), hbm()],
        out_specs=[vmem()] * (count + 1),
        scratch_shapes=[
            pltpu.VMEM(row_blocks.shape, jnp.int32),
            pltpu.VMEM((1, rows), jnp.int32),
            pltpu.VMEM((rows, width), bf16),
            pltpu.SemaphoreType.DMA((3,)),
        ],
        compiler_params=pltpu.CompilerParams(vmem_limit_bytes=8 * mib),
        name="dispatch",
    )(me, stay(row_blocks), stay(row_len.reshape(1, rows)), stay(queries))
    return got[0], got[1:]


tile_rows = 16


def attend_kernel(count, later, listed, group, long_blocks, scale_ref, kv, *refs):
    in_refs, refs = refs[:count], refs[count:]
    later_refs, refs = refs[:later], refs[later:]
    out_refs, refs = refs[:count], refs[count:]
    later_outs, refs = refs[:later], refs[later:]
    qs, os, lens, ints, scalars, later_sems, int_sem = refs
    copies = [pltpu.make_async_copy(later_refs[i], later_outs[i], later_sems.at[i]) for i in range(later)]
    for copy in copies:
        copy.start()
    slots = out_refs[0].shape[0]
    width = out_refs[0].shape[1]
    total = count * slots
    places = qs.shape[0]
    heads, tok, dim = kv.shape[2:]
    meta = jnp.concatenate([r[:, width : width + lanes] for r in in_refs], axis=0).astype(f32)
    lane = iota((total, lanes), 1)
    length = jnp.sum(
        jnp.where(lane == listed, meta * 64.0, jnp.where(lane == listed + 1, meta, 0.0)), axis=1, keepdims=True
    )
    ids = jnp.where(lane < listed, meta, 0.0)
    slot = iota((total, 1), 0).astype(f32)
    valid = length > 0.0
    big = float(total)

    def first_list(mask):
        first = jnp.min(jnp.where(mask, slot, big), axis=0, keepdims=True)
        return jnp.sum(jnp.where(slot == first, ids, 0.0), axis=0, keepdims=True)

    list_a = first_list(valid)
    same_a = jnp.sum(jnp.abs(ids - list_a), axis=1, keepdims=True) == 0.0
    in_a = valid & same_a
    in_b = valid & jnp.logical_not(same_a)
    list_b = first_list(in_b)
    span = float(2 * listed * tok)
    key = jnp.where(in_a, 2 * span + length, jnp.where(in_b, span + length, 0.0))
    key = key * total + (total - 1 - slot)
    eye = iota((total, total), 0) == iota((total, total), 1)
    key_row = jnp.sum(jnp.where(eye, key, 0.0), axis=0, keepdims=True)
    len_row = jnp.sum(jnp.where(eye, length, 0.0), axis=0, keepdims=True)
    rank = jnp.sum(jnp.where(key > key_row, 1.0, 0.0), axis=0, keepdims=True)
    a_row = key_row >= 2 * span * total
    b_row = jnp.logical_and(key_row >= span * total, jnp.logical_not(a_row))
    a_count = jnp.sum(jnp.where(a_row, 1.0, 0.0), axis=1, keepdims=True)
    a_tiles = jnp.floor((a_count + (tile_rows - 1)) * (1.0 / tile_rows))
    spot = jnp.where(a_row, rank, jnp.where(b_row, rank - a_count + a_tiles * tile_rows, float(places)))
    placed = iota((places, total), 0).astype(f32) == spot
    perm = jnp.where(placed, 1.0, 0.0).astype(bf16)
    len_sorted = jnp.sum(jnp.where(placed, len_row, 0.0), axis=1, keepdims=True)
    lens[...] = jnp.broadcast_to(len_sorted, (places, lanes)).astype(jnp.int32)
    tops = jnp.sum(
        jnp.where(iota((places, lanes), 0) == iota((places, lanes), 1) * tile_rows, len_sorted, 0.0),
        axis=0,
        keepdims=True,
    )
    row = iota((8, lanes), 0)
    ints[...] = jnp.where(
        row == 0, list_a, jnp.where(row == 1, list_b, jnp.where(row == 2, tops, a_tiles))
    ).astype(jnp.int32)
    int_copy = pltpu.make_async_copy(ints, scalars, int_sem)
    int_copy.start()
    queries = jnp.concatenate([r[:, 0:width] for r in in_refs], axis=0)
    qs[...] = mxu(perm, queries, (1, 0)).astype(bf16)
    os[...] = jnp.zeros_like(os)
    int_copy.wait()

    tall = group * tile_rows
    factors = [scale_ref[0, k] * (log2_e / math.sqrt(dim)) for k in range(heads)]
    short_blocks = max(1, long_blocks // 2)
    long_tokens, short_tokens = long_blocks * tok, short_blocks * tok

    def tile_body(t, _):
        top = scalars[2, t]
        doc = jnp.where(t >= scalars[3, 0], 1, 0)
        at = pl.multiple_of(t * tile_rows, tile_rows)
        spans = jnp.concatenate([lens[pl.ds(at, tile_rows), :]] * group, axis=0)[:, 0:1]
        qt = [
            jnp.concatenate(
                [qs[pl.ds(at, tile_rows), (k * group + g) * dim : (k * group + g + 1) * dim] for g in range(group)],
                axis=0,
            )
            for k in range(heads)
        ]

        def step(blocks_in, first, carry):
            keep = iota((tall, blocks_in * tok), 1) < spans - first * tok
            blocks = [scalars[doc, first + j] for j in range(blocks_in)]
            after = []
            for k in range(heads):
                peak, denom, acc = carry[k]
                keys = jnp.concatenate([kv[b, 0, k] for b in blocks], axis=0)
                scores = mxu(qt[k], keys, (1, 1)) * factors[k]
                scores = jnp.where(keep, scores, -1e30)
                higher = jnp.maximum(peak, jnp.max(scores, axis=1, keepdims=True))
                shrink = jnp.exp2(peak - higher)
                weights = jnp.exp2(scores - higher)
                denom = denom * shrink + jnp.sum(weights, axis=1, keepdims=True)
                values = jnp.concatenate([kv[b, 1, k] for b in blocks], axis=0)
                acc = acc * shrink + mxu(weights.astype(bf16), values, (1, 0))
                after.append((higher, denom, acc))
            return tuple(after)

        start = tuple(
            (jnp.full((tall, 1), -1e30, f32), jnp.zeros((tall, 1), f32), jnp.zeros((tall, dim), f32))
            for _ in range(heads)
        )
        longs = (top + (long_tokens - short_tokens - 1)) // long_tokens
        shorts = jnp.where(top > longs * long_tokens, 1, 0)

        @pl.when(top > 0)
        def _():
            done = lax.fori_loop(0, longs, lambda c, carry: step(long_blocks, c * long_blocks, carry), start)
            done = lax.fori_loop(0, shorts, lambda c, carry: step(short_blocks, longs * long_blocks, carry), done)
            for k in range(heads):
                _, denom, acc = done[k]
                out = (acc * (scale_ref[1, k] / denom)).astype(bf16)
                for g in range(group):
                    col = (k * group + g) * dim
                    os[pl.ds(at, tile_rows), col : col + dim] = out[g * tile_rows : (g + 1) * tile_rows]

        return 0

    lax.fori_loop(0, places // tile_rows, tile_body, 0)
    out = mxu(perm, os[...], (0, 0)).astype(bf16)
    for s in range(count):
        out_refs[s][...] = out[s * slots : (s + 1) * slots]
    for copy in copies:
        copy.wait()


def attend(received, kv_codes, kv_scale, later, listed, group):
    count = len(received)
    slots, wide = received[0].shape
    width = wide - lanes
    total = count * slots
    places = total + tile_rows
    got = pl.pallas_call(
        functools.partial(attend_kernel, count, len(later), listed, group, min(32, listed)),
        out_shape=[jax.ShapeDtypeStruct((slots, width), bf16)] * count
        + [pltpu.VMEM(a.shape, a.dtype) for a in later],
        in_specs=[smem()] + [vmem()] * (count + 1) + [hbm()] * len(later),
        out_specs=[vmem()] * (count + len(later)),
        scratch_shapes=[
            pltpu.VMEM((places, width), bf16),
            pltpu.VMEM((places, width), bf16),
            pltpu.VMEM((places, lanes), jnp.int32),
            pltpu.VMEM((8, lanes), jnp.int32),
            pltpu.SMEM((8, lanes), jnp.int32),
            pltpu.SemaphoreType.DMA((max(1, len(later)),)),
            pltpu.SemaphoreType.DMA,
        ],
        compiler_params=pltpu.CompilerParams(vmem_limit_bytes=12 * mib),
        name="attend",
    )(kv_scale, kv_codes, *received, *map(stay, later))
    return got[:count], got[count:]


def project_kernel(count, parts, at_ref, *refs):
    in_refs, w_ref = refs[:count], refs[count]
    own_ref, out_refs = refs[count + 1], refs[count + 2 : count + 1 + parts]
    x, y = refs[count + 1 + parts :]
    rows = in_refs[0].shape[0]
    piece = own_ref.shape[0]

    for s in range(count):
        source = at_ref[0] - s
        source = jnp.where(source < 0, source + count, source)
        x[pl.ds(pl.multiple_of(source * rows, rows), rows), :] = in_refs[s][...]
    cols = w_ref.shape[1]
    wide = 256 if cols % 256 == 0 else cols
    for c in range(0, cols, wide):
        y[:, c : c + wide] = mxu(x[...], w_ref[:, c : c + wide], (1, 0))
    for s in range(parts):
        target = at_ref[1] + s
        target = jnp.where(target >= parts, target - parts, target)
        value = y[pl.ds(pl.multiple_of(target * piece, piece), piece), :]
        if s == 0:
            own_ref[...] = value
        else:
            out_refs[s - 1][...] = value.astype(bf16)


def project(at, pieces, w_out, parts):
    count = len(pieces)
    rows, depth = pieces[0].shape
    cols = w_out.shape[1]
    tall = rows * count
    piece = tall // parts
    got = pl.pallas_call(
        functools.partial(project_kernel, count, parts),
        out_shape=[jax.ShapeDtypeStruct((piece, cols), f32)]
        + [jax.ShapeDtypeStruct((piece, cols), bf16)] * (parts - 1),
        in_specs=[smem()] + [vmem()] * (count + 1),
        out_specs=[vmem()] * parts,
        scratch_shapes=[pltpu.VMEM((tall, depth), bf16), pltpu.VMEM((tall, cols), f32)],
        compiler_params=pltpu.CompilerParams(vmem_limit_bytes=12 * mib),
        name="project",
    )(at, *pieces, w_out)
    return got[0], got[1:]


hidden_tile = 256


def swiglu_kernel(row_devs, head_devs, at_ref, gain_ref, *refs):
    pieces = refs[: row_devs * head_devs]
    gate_ref, up_ref, down_ref = refs[row_devs * head_devs : row_devs * head_devs + 3]
    outs = refs[row_devs * head_devs + 3 :]
    keep_refs, send_refs = outs[:row_devs], outs[row_devs : 2 * row_devs]
    x, inner, y = outs[2 * row_devs :]
    rows, cols = pieces[0].shape
    tall = x.shape[1]
    hidden = gate_ref.shape[1]
    steps = hidden // hidden_tile

    me_row, me_head = at_ref[0], at_ref[1]

    def flip(j):
        return me_head + (j & 1) * (1 - 2 * lax.rem(me_head, 2)) + (j & 2) * (1 - lax.rem(lax.div(me_head, 2), 2) * 2)

    def start_of(j):
        return pl.multiple_of(flip(j) * rows, rows)

    def behind(s):
        source = me_row - s
        return jnp.where(source < 0, source + row_devs, source)

    for s in range(row_devs):
        for j in range(head_devs):
            x[behind(s), pl.ds(start_of(j), rows), :] = pieces[s * head_devs + j][...]
    squares = jnp.zeros((tall, 1), f32)
    for z in range(row_devs):
        value = x[z].astype(f32)
        squares = squares + jnp.sum(value * value, axis=1, keepdims=True)
    inverse = lax.rsqrt(squares / (row_devs * cols) + norm_eps)
    for z in range(row_devs):
        x[z] = (x[z].astype(f32) * inverse * gain_ref[:, z * cols : (z + 1) * cols]).astype(bf16)

    for j in range(steps):
        cut = slice(j * hidden_tile, (j + 1) * hidden_tile)
        gate = jnp.zeros((tall, hidden_tile), f32)
        up = jnp.zeros((tall, hidden_tile), f32)
        for z in range(row_devs):
            gate = gate + mxu(x[z], gate_ref[z * cols : (z + 1) * cols, cut], (1, 0))
            up = up + mxu(x[z], up_ref[z * cols : (z + 1) * cols, cut], (1, 0))
        inner[:, cut] = (gate / (1.0 + jnp.exp(-gate)) * up).astype(bf16)

    for i in range(row_devs):
        @pl.loop(0, cols // hidden_tile)
        def _(t):
            cut = pl.ds(pl.multiple_of(t * hidden_tile, hidden_tile), hidden_tile)
            from_cut = pl.ds(pl.multiple_of(i * cols + t * hidden_tile, hidden_tile), hidden_tile)
            y[i, :, cut] = mxu(inner[...], down_ref[:, from_cut], (1, 0))

    for i in range(row_devs):
        target = me_row + i
        target = jnp.where(target >= row_devs, target - row_devs, target)
        for j in range(head_devs):
            value = y[target, pl.ds(start_of(j), rows), :]
            half = slice((j // 2) * rows, (j // 2 + 1) * rows)
            if j % 2 == 0:
                keep_refs[i][half, :] = value
            else:
                send_refs[i][half, :] = value.astype(bf16)


def swiglu(at, pieces, gain, w_gate, w_up, w_down, row_devs, head_devs):
    rows, cols = pieces[0].shape
    tall = rows * head_devs
    width, hidden = w_gate.shape
    half = rows * head_devs // 2
    got = pl.pallas_call(
        functools.partial(swiglu_kernel, row_devs, head_devs),
        out_shape=[jax.ShapeDtypeStruct((half, cols), f32)] * row_devs
        + [jax.ShapeDtypeStruct((half, cols), bf16)] * row_devs,
        in_specs=[smem(), vmem()] + [vmem()] * (len(pieces) + 3),
        out_specs=[vmem()] * (2 * row_devs),
        scratch_shapes=[
            pltpu.VMEM((row_devs, tall, cols), bf16),
            pltpu.VMEM((tall, hidden), bf16),
            pltpu.VMEM((row_devs, tall, cols), f32),
        ],
        compiler_params=pltpu.CompilerParams(vmem_limit_bytes=12 * mib),
        name="swiglu",
    )(at, gain.reshape(1, width), *pieces, w_gate, w_up, w_down)
    return got[:row_devs], got[row_devs:]


def shift(x, axis, step):
    n = lax.axis_size(axis)
    return lax.ppermute(x, axis, [(i, (i + step) % n) for i in range(n)])


def swap(x, axis, flip):
    return lax.ppermute(x, axis, [(i, i ^ flip) for i in range(lax.axis_size(axis))])


def feed_forward(at, hidden_state, norm_gain, w_gate, w_up, w_down):
    row_devs = lax.axis_size("rows")
    head_devs = lax.axis_size("heads")
    rows = hidden_state.shape[0]
    pieces = []
    for s in range(row_devs):
        piece = shift(hidden_state, "rows", s) if s else hidden_state
        across = swap(piece, "heads", 2)
        pieces += [piece, swap(piece, "heads", 1), across, swap(across, "heads", 1)]
    keeps, sends = swiglu(at, pieces, norm_gain, w_gate, w_up, w_down, row_devs, head_devs)
    total = hidden_state.astype(f32)
    order = sorted(range(row_devs), key=lambda i: (i == 0, abs(2 * i - row_devs)))
    for i in order:
        pair = keeps[i] + swap(sends[i], "heads", 1).astype(f32)
        part = pair[:rows] + swap(pair[rows:].astype(bf16), "heads", 2).astype(f32)
        total = total + (shift(part.astype(bf16), "rows", i).astype(f32) if i else part)
    return total.astype(bf16)


def feed_forward_gathered(hidden_state, norm_gain, w_gate, w_up, w_down):
    model_width = norm_gain.shape[0]
    full_rows = lax.all_gather(hidden_state, "rows", axis=1, tiled=True)
    every = lax.all_gather(full_rows, "heads", axis=0, tiled=True).astype(f32)
    totals = jnp.sum(every * every, axis=1)
    normed = (every * lax.rsqrt(totals / model_width + norm_eps)[:, None] * norm_gain).astype(bf16)
    gate = jnp.dot(normed, w_gate, preferred_element_type=f32)
    up = jnp.dot(normed, w_up, preferred_element_type=f32)
    inner = (jax.nn.silu(gate) * up).astype(bf16)
    partial_sum = jnp.dot(inner, w_down, preferred_element_type=f32).astype(bf16)
    section = lax.psum_scatter(partial_sum, "heads", scatter_dimension=0, tiled=True)
    ffn = lax.psum_scatter(section, "rows", scatter_dimension=1, tiled=True)
    return (hidden_state.astype(f32) + ffn.astype(f32)).astype(bf16)


def shards(
    resid, queries, kv_codes, kv_scale, row_blocks, row_len, w_out, norm_gain, w_gate, w_up, w_down
):
    row_devs = lax.axis_size("rows")
    head_devs = lax.axis_size("heads")
    rows_dev, width_q = queries.shape
    listed = row_blocks.shape[1]
    blocks_dev = kv_codes.shape[0]
    heads_dev, head_dim = kv_codes.shape[2], kv_codes.shape[4]
    group = width_q // (heads_dev * head_dim)
    capacity = max(2, 2 * rows_dev // row_devs)
    slots = -(-capacity // 16) * 16
    my_row = lax.axis_index("rows").astype(jnp.int32)
    my_head = lax.axis_index("heads").astype(jnp.int32)
    at = jnp.stack([my_row, my_head])

    place, sends = dispatch(at, queries, row_blocks, row_len, row_devs, slots, blocks_dev)
    received = [sends[0]] + [shift(sends[s], "rows", s) for s in range(1, row_devs)]
    (kv_near,) = fetch(place, kv_codes)
    results, (w_gate, w_out) = attend(received, kv_near, kv_scale, (w_gate, w_out), listed, group)
    back = [results[0]] + [shift(results[s], "rows", -s) for s in range(1, row_devs)]
    attended = jnp.dot(place, jnp.concatenate(back, axis=0), preferred_element_type=f32).astype(bf16)
    pieces = [attended] + [shift(attended, "rows", s) for s in range(1, row_devs)]
    pieces, w_up, w_down = lax.optimization_barrier((pieces, *fetch(attended, w_up, w_down)))
    own, others = project(at, pieces, w_out, head_devs)
    attn_out = own
    for s in range(1, head_devs):
        attn_out = attn_out + shift(others[s - 1], "heads", s).astype(f32)
    hidden_state = (resid.astype(f32) + attn_out).astype(bf16)

    if head_devs == 4 and hidden_state.shape[1] % hidden_tile == 0:
        return feed_forward(at, hidden_state, norm_gain, w_gate, w_up, w_down)
    return feed_forward_gathered(hidden_state, norm_gain, w_gate, w_up, w_down)


def solution(mesh):
    placed = (
        P(("groups", "heads"), "rows"),
        P(("groups", "rows"), "heads"),
        P(("groups", "rows"), None, "heads", None, None),
        P("groups", "heads"),
        P(("groups", "rows"), None),
        P(("groups", "rows")),
        P("heads", "rows"),
        P(),
        P(None, ("rows", "heads")),
        P(None, ("rows", "heads")),
        P(("rows", "heads"), None),
    )
    return jax.shard_map(
        shards,
        mesh=mesh,
        in_specs=placed,
        out_specs=P(("groups", "heads"), "rows"),
        check_vma=False,
    )
```

```python
import functools
import math

import jax
import jax.numpy as jnp
from jax import lax
from jax.experimental import pallas as pl
from jax.experimental.pallas import tpu as pltpu
from jax.sharding import PartitionSpec as P

norm_eps = 1e-06
log2_e = 1.4426950408889634
mib = 1 << 20
lanes = 128
f32 = jnp.float32
bf16 = jnp.bfloat16

vmem = functools.partial(pl.BlockSpec, memory_space=pltpu.VMEM)
smem = functools.partial(pl.BlockSpec, memory_space=pltpu.SMEM)
hbm = functools.partial(pl.BlockSpec, memory_space=pltpu.HBM)


def stay(x):
    return pltpu.with_memory_space_constraint(x, pltpu.HBM)


def iota(shape, dim):
    return lax.broadcasted_iota(jnp.int32, shape, dim)


def mxu(a, b, contract):
    return lax.dot_general(a, b, ((contract[:1], contract[1:]), ((), ())), preferred_element_type=f32)


def fetch_kernel(count, after_ref, *refs):
    sources, targets, sems = refs[:count], refs[count : 2 * count], refs[2 * count]
    copies = [pltpu.make_async_copy(sources[i], targets[i], sems.at[i]) for i in range(count)]
    for copy in copies:
        copy.start()
    for copy in copies:
        copy.wait()


def fetch(after, *arrays):
    count = len(arrays)
    return pl.pallas_call(
        functools.partial(fetch_kernel, count),
        out_shape=[pltpu.VMEM(a.shape, a.dtype) for a in arrays],
        in_specs=[pl.BlockSpec(memory_space=pl.ANY)] + [hbm()] * count,
        out_specs=[vmem()] * count,
        scratch_shapes=[pltpu.SemaphoreType.DMA((count,))],
        cost_estimate=pl.CostEstimate(
            flops=0, bytes_accessed=sum(a.size * a.dtype.itemsize for a in arrays), transcendentals=0
        ),
        compiler_params=pltpu.CompilerParams(vmem_limit_bytes=1 * mib),
        name="fetch",
    )(after, *map(stay, arrays))


def dispatch_kernel(blocks_dev, me_ref, ids_hbm, len_hbm, q_hbm, place_ref, *refs):
    send_refs, (ids_ref, len_ref, q_ref, sems) = refs[:-4], refs[-4:]
    ids_copy = pltpu.make_async_copy(ids_hbm, ids_ref, sems.at[0])
    len_copy = pltpu.make_async_copy(len_hbm, len_ref, sems.at[1])
    q_copy = pltpu.make_async_copy(q_hbm, q_ref, sems.at[2])
    for copy in (ids_copy, len_copy, q_copy):
        copy.start()
    count = len(send_refs)
    slots = send_refs[0].shape[0]
    width = q_ref.shape[1]
    rows, listed = ids_ref.shape
    me = me_ref[0]
    ids_copy.wait()
    len_copy.wait()
    ids = ids_ref[...].astype(f32)
    owner = jnp.floor((ids[:, 0:1] + 0.5) * (1.0 / blocks_dev))
    ahead = owner - me.astype(f32)
    ahead = jnp.where(ahead < 0, ahead + count, ahead)
    lane = iota((rows, lanes), 1)
    hot = jnp.where(lane.astype(f32) == ahead, 1.0, 0.0)
    lower = jnp.where(iota((rows, rows), 1) < iota((rows, rows), 0), 1.0, 0.0)
    before = mxu(lower.astype(bf16), hot.astype(bf16), (1, 0))
    rank = jnp.sum(before * hot, axis=1, keepdims=True)
    target = ahead * slots + rank
    place = jnp.where(iota((rows, count * slots), 1).astype(f32) == target, 1.0, 0.0).astype(bf16)
    place_ref[...] = place
    local = (ids - owner * blocks_dev).astype(bf16)
    eye = jnp.where(iota((listed, lanes), 0) == iota((listed, lanes), 1), 1.0, 0.0).astype(bf16)
    meta = mxu(local, eye, (1, 0))
    spread = jnp.broadcast_to(len_ref[...].astype(f32), (rows, rows))
    length = jnp.sum(
        jnp.where(iota((rows, rows), 0) == iota((rows, rows), 1), spread, 0.0), axis=1, keepdims=True
    )
    high = jnp.floor(length * (1.0 / 64))
    meta = jnp.where(lane == listed, high, meta)
    meta = jnp.where(lane == listed + 1, length - high * 64, meta)
    q_copy.wait()
    send = mxu(place, q_ref[...], (0, 0)).astype(bf16)
    send_meta = mxu(place, meta.astype(bf16), (0, 0)).astype(bf16)
    for s in range(count):
        send_refs[s][:, 0:width] = send[s * slots : (s + 1) * slots]
        send_refs[s][:, width : width + lanes] = send_meta[s * slots : (s + 1) * slots]


def dispatch(me, queries, row_blocks, row_len, count, slots, blocks_dev):
    rows, width = queries.shape
    outs = [jax.ShapeDtypeStruct((rows, count * slots), bf16)]
    outs += [jax.ShapeDtypeStruct((slots, width + lanes), bf16)] * count
    got = pl.pallas_call(
        functools.partial(dispatch_kernel, blocks_dev),
        out_shape=outs,
        in_specs=[smem(), hbm(), hbm(), hbm()],
        out_specs=[vmem()] * (count + 1),
        scratch_shapes=[
            pltpu.VMEM(row_blocks.shape, jnp.int32),
            pltpu.VMEM((1, rows), jnp.int32),
            pltpu.VMEM((rows, width), bf16),
            pltpu.SemaphoreType.DMA((3,)),
        ],
        compiler_params=pltpu.CompilerParams(vmem_limit_bytes=8 * mib),
        name="dispatch",
    )(me, stay(row_blocks), stay(row_len.reshape(1, rows)), stay(queries))
    return got[0], got[1:]


tile_rows = 16


def attend_kernel(count, later, listed, group, long_blocks, scale_ref, kv, *refs):
    in_refs, refs = refs[:count], refs[count:]
    later_refs, refs = refs[:later], refs[later:]
    out_refs, refs = refs[:count], refs[count:]
    later_outs, refs = refs[:later], refs[later:]
    qs, os, lens, ints, scalars, later_sems, int_sem = refs
    copies = [pltpu.make_async_copy(later_refs[i], later_outs[i], later_sems.at[i]) for i in range(later)]
    for copy in copies:
        copy.start()
    slots = out_refs[0].shape[0]
    width = out_refs[0].shape[1]
    total = count * slots
    places = qs.shape[0]
    heads, tok, dim = kv.shape[2:]
    meta = jnp.concatenate([r[:, width : width + lanes] for r in in_refs], axis=0).astype(f32)
    lane = iota((total, lanes), 1)
    length = jnp.sum(
        jnp.where(lane == listed, meta * 64.0, jnp.where(lane == listed + 1, meta, 0.0)), axis=1, keepdims=True
    )
    ids = jnp.where(lane < listed, meta, 0.0)
    slot = iota((total, 1), 0).astype(f32)
    valid = length > 0.0
    big = float(total)

    def first_list(mask):
        first = jnp.min(jnp.where(mask, slot, big), axis=0, keepdims=True)
        return jnp.sum(jnp.where(slot == first, ids, 0.0), axis=0, keepdims=True)

    list_a = first_list(valid)
    same_a = jnp.sum(jnp.abs(ids - list_a), axis=1, keepdims=True) == 0.0
    in_a = valid & same_a
    in_b = valid & jnp.logical_not(same_a)
    list_b = first_list(in_b)
    span = float(2 * listed * tok)
    key = jnp.where(in_a, 2 * span + length, jnp.where(in_b, span + length, 0.0))
    key = key * total + (total - 1 - slot)
    eye = iota((total, total), 0) == iota((total, total), 1)
    key_row = jnp.sum(jnp.where(eye, key, 0.0), axis=0, keepdims=True)
    len_row = jnp.sum(jnp.where(eye, length, 0.0), axis=0, keepdims=True)
    rank = jnp.sum(jnp.where(key > key_row, 1.0, 0.0), axis=0, keepdims=True)
    a_row = key_row >= 2 * span * total
    b_row = jnp.logical_and(key_row >= span * total, jnp.logical_not(a_row))
    a_count = jnp.sum(jnp.where(a_row, 1.0, 0.0), axis=1, keepdims=True)
    a_tiles = jnp.floor((a_count + (tile_rows - 1)) * (1.0 / tile_rows))
    spot = jnp.where(a_row, rank, jnp.where(b_row, rank - a_count + a_tiles * tile_rows, float(places)))
    placed = iota((places, total), 0).astype(f32) == spot
    perm = jnp.where(placed, 1.0, 0.0).astype(bf16)
    len_sorted = jnp.sum(jnp.where(placed, len_row, 0.0), axis=1, keepdims=True)
    lens[...] = jnp.broadcast_to(len_sorted, (places, lanes)).astype(jnp.int32)
    tops = jnp.sum(
        jnp.where(iota((places, lanes), 0) == iota((places, lanes), 1) * tile_rows, len_sorted, 0.0),
        axis=0,
        keepdims=True,
    )
    row = iota((8, lanes), 0)
    ints[...] = jnp.where(
        row == 0, list_a, jnp.where(row == 1, list_b, jnp.where(row == 2, tops, a_tiles))
    ).astype(jnp.int32)
    int_copy = pltpu.make_async_copy(ints, scalars, int_sem)
    int_copy.start()
    queries = jnp.concatenate([r[:, 0:width] for r in in_refs], axis=0)
    qs[...] = mxu(perm, queries, (1, 0)).astype(bf16)
    os[...] = jnp.zeros_like(os)
    int_copy.wait()

    tall = group * tile_rows
    factors = [scale_ref[0, k] * (log2_e / math.sqrt(dim)) for k in range(heads)]
    short_blocks = max(1, long_blocks // 2)
    long_tokens, short_tokens = long_blocks * tok, short_blocks * tok

    def tile_body(t, _):
        top = scalars[2, t]
        doc = jnp.where(t >= scalars[3, 0], 1, 0)
        at = pl.multiple_of(t * tile_rows, tile_rows)
        spans = jnp.concatenate([lens[pl.ds(at, tile_rows), :]] * group, axis=0)[:, 0:1]
        qt = [
            jnp.concatenate(
                [qs[pl.ds(at, tile_rows), (k * group + g) * dim : (k * group + g + 1) * dim] for g in range(group)],
                axis=0,
            )
            for k in range(heads)
        ]

        def step(blocks_in, first, carry):
            keep = iota((tall, blocks_in * tok), 1) < spans - first * tok
            blocks = [scalars[doc, first + j] for j in range(blocks_in)]
            after = []
            for k in range(heads):
                peak, denom, acc = carry[k]
                keys = jnp.concatenate([kv[b, 0, k] for b in blocks], axis=0)
                scores = mxu(qt[k], keys, (1, 1)) * factors[k]
                scores = jnp.where(keep, scores, -1e30)
                higher = jnp.maximum(peak, jnp.max(scores, axis=1, keepdims=True))
                shrink = jnp.exp2(peak - higher)
                weights = jnp.exp2(scores - higher)
                denom = denom * shrink + jnp.sum(weights, axis=1, keepdims=True)
                values = jnp.concatenate([kv[b, 1, k] for b in blocks], axis=0)
                acc = acc * shrink + mxu(weights.astype(bf16), values, (1, 0))
                after.append((higher, denom, acc))
            return tuple(after)

        start = tuple(
            (jnp.full((tall, 1), -1e30, f32), jnp.zeros((tall, 1), f32), jnp.zeros((tall, dim), f32))
            for _ in range(heads)
        )
        longs = (top + (long_tokens - short_tokens - 1)) // long_tokens
        shorts = jnp.where(top > longs * long_tokens, 1, 0)

        @pl.when(top > 0)
        def _():
            done = lax.fori_loop(0, longs, lambda c, carry: step(long_blocks, c * long_blocks, carry), start)
            done = lax.fori_loop(0, shorts, lambda c, carry: step(short_blocks, longs * long_blocks, carry), done)
            for k in range(heads):
                _, denom, acc = done[k]
                out = (acc * (scale_ref[1, k] / denom)).astype(bf16)
                for g in range(group):
                    col = (k * group + g) * dim
                    os[pl.ds(at, tile_rows), col : col + dim] = out[g * tile_rows : (g + 1) * tile_rows]

        return 0

    lax.fori_loop(0, places // tile_rows, tile_body, 0)
    out = mxu(perm, os[...], (0, 0)).astype(bf16)
    for s in range(count):
        out_refs[s][...] = out[s * slots : (s + 1) * slots]
    for copy in copies:
        copy.wait()


def attend(received, kv_codes, kv_scale, later, listed, group):
    count = len(received)
    slots, wide = received[0].shape
    width = wide - lanes
    total = count * slots
    places = total + tile_rows
    got = pl.pallas_call(
        functools.partial(attend_kernel, count, len(later), listed, group, min(32, listed)),
        out_shape=[jax.ShapeDtypeStruct((slots, width), bf16)] * count
        + [pltpu.VMEM(a.shape, a.dtype) for a in later],
        in_specs=[smem()] + [vmem()] * (count + 1) + [hbm()] * len(later),
        out_specs=[vmem()] * (count + len(later)),
        scratch_shapes=[
            pltpu.VMEM((places, width), bf16),
            pltpu.VMEM((places, width), bf16),
            pltpu.VMEM((places, lanes), jnp.int32),
            pltpu.VMEM((8, lanes), jnp.int32),
            pltpu.SMEM((8, lanes), jnp.int32),
            pltpu.SemaphoreType.DMA((max(1, len(later)),)),
            pltpu.SemaphoreType.DMA,
        ],
        compiler_params=pltpu.CompilerParams(vmem_limit_bytes=12 * mib),
        name="attend",
    )(kv_scale, kv_codes, *received, *map(stay, later))
    return got[:count], got[count:]


def project_kernel(count, parts, at_ref, *refs):
    in_refs, w_ref = refs[:count], refs[count]
    own_ref, out_refs = refs[count + 1], refs[count + 2 : count + 1 + parts]
    x, y = refs[count + 1 + parts :]
    rows = in_refs[0].shape[0]
    piece = own_ref.shape[0]

    for s in range(count):
        source = at_ref[0] - s
        source = jnp.where(source < 0, source + count, source)
        x[pl.ds(pl.multiple_of(source * rows, rows), rows), :] = in_refs[s][...]
    cols = w_ref.shape[1]
    wide = 256 if cols % 256 == 0 else cols
    for c in range(0, cols, wide):
        y[:, c : c + wide] = mxu(x[...], w_ref[:, c : c + wide], (1, 0))
    for s in range(parts):
        target = at_ref[1] + s
        target = jnp.where(target >= parts, target - parts, target)
        value = y[pl.ds(pl.multiple_of(target * piece, piece), piece), :]
        if s == 0:
            own_ref[...] = value
        else:
            out_refs[s - 1][...] = value.astype(bf16)


def project(at, pieces, w_out, parts):
    count = len(pieces)
    rows, depth = pieces[0].shape
    cols = w_out.shape[1]
    tall = rows * count
    piece = tall // parts
    got = pl.pallas_call(
        functools.partial(project_kernel, count, parts),
        out_shape=[jax.ShapeDtypeStruct((piece, cols), f32)]
        + [jax.ShapeDtypeStruct((piece, cols), bf16)] * (parts - 1),
        in_specs=[smem()] + [vmem()] * (count + 1),
        out_specs=[vmem()] * parts,
        scratch_shapes=[pltpu.VMEM((tall, depth), bf16), pltpu.VMEM((tall, cols), f32)],
        compiler_params=pltpu.CompilerParams(vmem_limit_bytes=12 * mib),
        name="project",
    )(at, *pieces, w_out)
    return got[0], got[1:]


hidden_tile = 256


def swiglu_kernel(row_devs, head_devs, at_ref, gain_ref, *refs):
    count = row_devs * head_devs
    pieces, refs = refs[:count], refs[count:]
    gate_ref, up_ref, down_ref = refs[:3]
    keep_refs, send_refs = refs[3 : 3 + row_devs], refs[3 + row_devs : 3 + 2 * row_devs]
    x, inner = refs[3 + 2 * row_devs :]
    rows, cols = pieces[0].shape
    tall, hidden = inner.shape
    width = row_devs * cols
    order = [*range(0, head_devs, 2), *range(1, head_devs, 2)]

    def turned(n):
        n = at_ref[0] + n % row_devs
        n = jnp.where(n >= row_devs, n - row_devs, n)
        return pl.multiple_of(n * cols, cols)

    for at, j in enumerate(order):
        values = [pieces[s * head_devs + j][...].astype(f32) for s in range(row_devs)]
        squares = sum(jnp.sum(v * v, axis=1, keepdims=True) for v in values)
        inverse = lax.rsqrt(squares / width + norm_eps)
        for s in range(row_devs):
            value = values[s] * inverse * gain_ref[:, pl.ds(turned(-s), cols)]
            x[s, at * rows : (at + 1) * rows, :] = value.astype(bf16)

    for c in range(0, hidden, hidden_tile):
        cut = slice(c, c + hidden_tile)
        gate = jnp.zeros((tall, hidden_tile), f32)
        up = jnp.zeros((tall, hidden_tile), f32)
        for s in range(row_devs):
            gate = gate + mxu(x[s], gate_ref[pl.ds(turned(-s), cols), cut], (1, 0))
            up = up + mxu(x[s], up_ref[pl.ds(turned(-s), cols), cut], (1, 0))
        inner[:, cut] = (gate / (1.0 + jnp.exp(-gate)) * up).astype(bf16)

    for i in range(row_devs):
        for c in range(0, cols, hidden_tile):
            cut = slice(c, c + hidden_tile)
            y = mxu(inner[...], down_ref[:, pl.ds(pl.multiple_of(turned(i) + c, hidden_tile), hidden_tile)], (1, 0))
            keep_refs[i][:, cut] = y[: tall // 2]
            send_refs[i][:, cut] = y[tall // 2 :].astype(bf16)


def swiglu(at, pieces, gain, w_gate, w_up, w_down, row_devs, head_devs):
    rows, cols = pieces[0].shape
    tall = rows * head_devs
    width, hidden = w_gate.shape
    half = rows * head_devs // 2
    got = pl.pallas_call(
        functools.partial(swiglu_kernel, row_devs, head_devs),
        out_shape=[jax.ShapeDtypeStruct((half, cols), f32)] * row_devs
        + [jax.ShapeDtypeStruct((half, cols), bf16)] * row_devs,
        in_specs=[smem(), vmem()] + [vmem()] * (len(pieces) + 3),
        out_specs=[vmem()] * (2 * row_devs),
        scratch_shapes=[
            pltpu.VMEM((row_devs, tall, cols), bf16),
            pltpu.VMEM((tall, hidden), bf16),
        ],
        compiler_params=pltpu.CompilerParams(vmem_limit_bytes=12 * mib),
        name="swiglu",
    )(at, gain.reshape(1, width), *pieces, w_gate, w_up, w_down)
    return got[:row_devs], got[row_devs:]


def shift(x, axis, step):
    n = lax.axis_size(axis)
    return lax.ppermute(x, axis, [(i, (i + step) % n) for i in range(n)])


def swap(x, axis, flip):
    return lax.ppermute(x, axis, [(i, i ^ flip) for i in range(lax.axis_size(axis))])


def feed_forward(at, hidden_state, norm_gain, w_gate, w_up, w_down):
    row_devs = lax.axis_size("rows")
    head_devs = lax.axis_size("heads")
    rows = hidden_state.shape[0]
    pieces = []
    for s in range(row_devs):
        piece = shift(hidden_state, "rows", s) if s else hidden_state
        across = swap(piece, "heads", 2)
        pieces += [piece, swap(piece, "heads", 1), across, swap(across, "heads", 1)]
    keeps, sends = swiglu(at, pieces, norm_gain, w_gate, w_up, w_down, row_devs, head_devs)
    total = hidden_state.astype(f32)
    order = sorted(range(row_devs), key=lambda i: (i == 0, abs(2 * i - row_devs)))
    for i in order:
        pair = keeps[i] + swap(sends[i], "heads", 1).astype(f32)
        part = pair[:rows] + swap(pair[rows:].astype(bf16), "heads", 2).astype(f32)
        total = total + (shift(part.astype(bf16), "rows", i).astype(f32) if i else part)
    return total.astype(bf16)


def feed_forward_gathered(hidden_state, norm_gain, w_gate, w_up, w_down):
    model_width = norm_gain.shape[0]
    full_rows = lax.all_gather(hidden_state, "rows", axis=1, tiled=True)
    every = lax.all_gather(full_rows, "heads", axis=0, tiled=True).astype(f32)
    totals = jnp.sum(every * every, axis=1)
    normed = (every * lax.rsqrt(totals / model_width + norm_eps)[:, None] * norm_gain).astype(bf16)
    gate = jnp.dot(normed, w_gate, preferred_element_type=f32)
    up = jnp.dot(normed, w_up, preferred_element_type=f32)
    inner = (jax.nn.silu(gate) * up).astype(bf16)
    partial_sum = jnp.dot(inner, w_down, preferred_element_type=f32).astype(bf16)
    section = lax.psum_scatter(partial_sum, "heads", scatter_dimension=0, tiled=True)
    ffn = lax.psum_scatter(section, "rows", scatter_dimension=1, tiled=True)
    return (hidden_state.astype(f32) + ffn.astype(f32)).astype(bf16)


def shards(
    resid, queries, kv_codes, kv_scale, row_blocks, row_len, w_out, norm_gain, w_gate, w_up, w_down
):
    row_devs = lax.axis_size("rows")
    head_devs = lax.axis_size("heads")
    rows_dev, width_q = queries.shape
    listed = row_blocks.shape[1]
    blocks_dev = kv_codes.shape[0]
    heads_dev, head_dim = kv_codes.shape[2], kv_codes.shape[4]
    group = width_q // (heads_dev * head_dim)
    capacity = max(2, 2 * rows_dev // row_devs)
    slots = -(-capacity // 16) * 16
    my_row = lax.axis_index("rows").astype(jnp.int32)
    my_head = lax.axis_index("heads").astype(jnp.int32)
    at = jnp.stack([my_row, my_head])

    place, sends = dispatch(at, queries, row_blocks, row_len, row_devs, slots, blocks_dev)
    received = [sends[0]] + [shift(sends[s], "rows", s) for s in range(1, row_devs)]
    (kv_near,) = fetch(place, kv_codes)
    results, (w_gate, w_out) = attend(received, kv_near, kv_scale, (w_gate, w_out), listed, group)
    back = [results[0]] + [shift(results[s], "rows", -s) for s in range(1, row_devs)]
    attended = jnp.dot(place, jnp.concatenate(back, axis=0), preferred_element_type=f32).astype(bf16)
    pieces = [attended] + [shift(attended, "rows", s) for s in range(1, row_devs)]
    pieces, w_up, w_down = lax.optimization_barrier((pieces, *fetch(attended, w_up, w_down)))
    own, others = project(at, pieces, w_out, head_devs)
    attn_out = own
    for s in range(1, head_devs):
        attn_out = attn_out + shift(others[s - 1], "heads", s).astype(f32)
    hidden_state = (resid.astype(f32) + attn_out).astype(bf16)

    if head_devs == 4 and hidden_state.shape[1] % hidden_tile == 0:
        return feed_forward(at, hidden_state, norm_gain, w_gate, w_up, w_down)
    return feed_forward_gathered(hidden_state, norm_gain, w_gate, w_up, w_down)


def solution(mesh):
    placed = (
        P(("groups", "heads"), "rows"),
        P(("groups", "rows"), "heads"),
        P(("groups", "rows"), None, "heads", None, None),
        P("groups", "heads"),
        P(("groups", "rows"), None),
        P(("groups", "rows")),
        P("heads", "rows"),
        P(),
        P(None, ("rows", "heads")),
        P(None, ("rows", "heads")),
        P(("rows", "heads"), None),
    )
    return jax.shard_map(
        shards,
        mesh=mesh,
        in_specs=placed,
        out_specs=P(("groups", "heads"), "rows"),
        check_vma=False,
    )
```

```python
import functools
import math

import jax
import jax.numpy as jnp
from jax import lax
from jax.experimental import pallas as pl
from jax.experimental.pallas import tpu as pltpu
from jax.sharding import PartitionSpec as P

norm_eps = 1e-06
log2_e = 1.4426950408889634
mib = 1 << 20
lanes = 128
f32 = jnp.float32
bf16 = jnp.bfloat16

vmem = functools.partial(pl.BlockSpec, memory_space=pltpu.VMEM)
smem = functools.partial(pl.BlockSpec, memory_space=pltpu.SMEM)
hbm = functools.partial(pl.BlockSpec, memory_space=pltpu.HBM)


def stay(x):
    return pltpu.with_memory_space_constraint(x, pltpu.HBM)


def iota(shape, dim):
    return lax.broadcasted_iota(jnp.int32, shape, dim)


def mxu(a, b, contract):
    return lax.dot_general(a, b, ((contract[:1], contract[1:]), ((), ())), preferred_element_type=f32)


def fetch_kernel(count, after_ref, *refs):
    sources, targets, sems = refs[:count], refs[count : 2 * count], refs[2 * count]
    copies = [pltpu.make_async_copy(sources[i], targets[i], sems.at[i]) for i in range(count)]
    for copy in copies:
        copy.start()
    for copy in copies:
        copy.wait()


def fetch(after, *arrays):
    count = len(arrays)
    return pl.pallas_call(
        functools.partial(fetch_kernel, count),
        out_shape=[pltpu.VMEM(a.shape, a.dtype) for a in arrays],
        in_specs=[pl.BlockSpec(memory_space=pl.ANY)] + [hbm()] * count,
        out_specs=[vmem()] * count,
        scratch_shapes=[pltpu.SemaphoreType.DMA((count,))],
        cost_estimate=pl.CostEstimate(
            flops=0, bytes_accessed=sum(a.size * a.dtype.itemsize for a in arrays), transcendentals=0
        ),
        compiler_params=pltpu.CompilerParams(vmem_limit_bytes=1 * mib),
        name="fetch",
    )(after, *map(stay, arrays))


def dispatch_kernel(blocks_dev, me_ref, ids_hbm, len_hbm, q_hbm, place_ref, *refs):
    send_refs, (ids_ref, len_ref, q_ref, sems) = refs[:-4], refs[-4:]
    ids_copy = pltpu.make_async_copy(ids_hbm, ids_ref, sems.at[0])
    len_copy = pltpu.make_async_copy(len_hbm, len_ref, sems.at[1])
    q_copy = pltpu.make_async_copy(q_hbm, q_ref, sems.at[2])
    for copy in (ids_copy, len_copy, q_copy):
        copy.start()
    count = len(send_refs)
    slots = send_refs[0].shape[0]
    width = q_ref.shape[1]
    rows, listed = ids_ref.shape
    me = me_ref[0]
    ids_copy.wait()
    len_copy.wait()
    ids = ids_ref[...].astype(f32)
    owner = jnp.floor((ids[:, 0:1] + 0.5) * (1.0 / blocks_dev))
    ahead = owner - me.astype(f32)
    ahead = jnp.where(ahead < 0, ahead + count, ahead)
    lane = iota((rows, lanes), 1)
    hot = jnp.where(lane.astype(f32) == ahead, 1.0, 0.0)
    lower = jnp.where(iota((rows, rows), 1) < iota((rows, rows), 0), 1.0, 0.0)
    before = mxu(lower.astype(bf16), hot.astype(bf16), (1, 0))
    rank = jnp.sum(before * hot, axis=1, keepdims=True)
    target = ahead * slots + rank
    place = jnp.where(iota((rows, count * slots), 1).astype(f32) == target, 1.0, 0.0).astype(bf16)
    place_ref[...] = place
    local = (ids - owner * blocks_dev).astype(bf16)
    eye = jnp.where(iota((listed, lanes), 0) == iota((listed, lanes), 1), 1.0, 0.0).astype(bf16)
    meta = mxu(local, eye, (1, 0))
    spread = jnp.broadcast_to(len_ref[...].astype(f32), (rows, rows))
    length = jnp.sum(
        jnp.where(iota((rows, rows), 0) == iota((rows, rows), 1), spread, 0.0), axis=1, keepdims=True
    )
    high = jnp.floor(length * (1.0 / 64))
    meta = jnp.where(lane == listed, high, meta)
    meta = jnp.where(lane == listed + 1, length - high * 64, meta)
    q_copy.wait()
    send = mxu(place, q_ref[...], (0, 0)).astype(bf16)
    send_meta = mxu(place, meta.astype(bf16), (0, 0)).astype(bf16)
    for s in range(count):
        send_refs[s][:, 0:width] = send[s * slots : (s + 1) * slots]
        send_refs[s][:, width : width + lanes] = send_meta[s * slots : (s + 1) * slots]


def dispatch(me, queries, row_blocks, row_len, count, slots, blocks_dev):
    rows, width = queries.shape
    outs = [jax.ShapeDtypeStruct((rows, count * slots), bf16)]
    outs += [jax.ShapeDtypeStruct((slots, width + lanes), bf16)] * count
    got = pl.pallas_call(
        functools.partial(dispatch_kernel, blocks_dev),
        out_shape=outs,
        in_specs=[smem(), hbm(), hbm(), hbm()],
        out_specs=[vmem()] * (count + 1),
        scratch_shapes=[
            pltpu.VMEM(row_blocks.shape, jnp.int32),
            pltpu.VMEM((1, rows), jnp.int32),
            pltpu.VMEM((rows, width), bf16),
            pltpu.SemaphoreType.DMA((3,)),
        ],
        compiler_params=pltpu.CompilerParams(vmem_limit_bytes=8 * mib),
        name="dispatch",
    )(me, stay(row_blocks), stay(row_len.reshape(1, rows)), stay(queries))
    return got[0], got[1:]


tile_rows = 16


def attend_kernel(count, later, listed, group, long_blocks, scale_ref, kv, *refs):
    in_refs, refs = refs[:count], refs[count:]
    later_refs, refs = refs[:later], refs[later:]
    out_refs, refs = refs[:count], refs[count:]
    later_outs, refs = refs[:later], refs[later:]
    qs, os, lens, ints, scalars, later_sems, int_sem = refs
    copies = [pltpu.make_async_copy(later_refs[i], later_outs[i], later_sems.at[i]) for i in range(later)]
    for copy in copies:
        copy.start()
    slots = out_refs[0].shape[0]
    width = out_refs[0].shape[1]
    total = count * slots
    places = qs.shape[0]
    heads, tok, dim = kv.shape[2:]
    meta = jnp.concatenate([r[:, width : width + lanes] for r in in_refs], axis=0).astype(f32)
    lane = iota((total, lanes), 1)
    length = jnp.sum(
        jnp.where(lane == listed, meta * 64.0, jnp.where(lane == listed + 1, meta, 0.0)), axis=1, keepdims=True
    )
    ids = jnp.where(lane < listed, meta, 0.0)
    slot = iota((total, 1), 0).astype(f32)
    valid = length > 0.0
    big = float(total)

    def first_list(mask):
        first = jnp.min(jnp.where(mask, slot, big), axis=0, keepdims=True)
        return jnp.sum(jnp.where(slot == first, ids, 0.0), axis=0, keepdims=True)

    list_a = first_list(valid)
    same_a = jnp.sum(jnp.abs(ids - list_a), axis=1, keepdims=True) == 0.0
    in_a = valid & same_a
    in_b = valid & jnp.logical_not(same_a)
    list_b = first_list(in_b)
    span = float(2 * listed * tok)
    key = jnp.where(in_a, 2 * span + length, jnp.where(in_b, span + length, 0.0))
    key = key * total + (total - 1 - slot)
    eye = iota((total, total), 0) == iota((total, total), 1)
    key_row = jnp.sum(jnp.where(eye, key, 0.0), axis=0, keepdims=True)
    len_row = jnp.sum(jnp.where(eye, length, 0.0), axis=0, keepdims=True)
    rank = jnp.sum(jnp.where(key > key_row, 1.0, 0.0), axis=0, keepdims=True)
    a_row = key_row >= 2 * span * total
    b_row = jnp.logical_and(key_row >= span * total, jnp.logical_not(a_row))
    a_count = jnp.sum(jnp.where(a_row, 1.0, 0.0), axis=1, keepdims=True)
    a_tiles = jnp.floor((a_count + (tile_rows - 1)) * (1.0 / tile_rows))
    spot = jnp.where(a_row, rank, jnp.where(b_row, rank - a_count + a_tiles * tile_rows, float(places)))
    placed = iota((places, total), 0).astype(f32) == spot
    perm = jnp.where(placed, 1.0, 0.0).astype(bf16)
    len_sorted = jnp.sum(jnp.where(placed, len_row, 0.0), axis=1, keepdims=True)
    lens[...] = jnp.broadcast_to(len_sorted, (places, lanes)).astype(jnp.int32)
    tops = jnp.sum(
        jnp.where(iota((places, lanes), 0) == iota((places, lanes), 1) * tile_rows, len_sorted, 0.0),
        axis=0,
        keepdims=True,
    )
    row = iota((8, lanes), 0)
    ints[...] = jnp.where(
        row == 0, list_a, jnp.where(row == 1, list_b, jnp.where(row == 2, tops, a_tiles))
    ).astype(jnp.int32)
    int_copy = pltpu.make_async_copy(ints, scalars, int_sem)
    int_copy.start()
    queries = jnp.concatenate([r[:, 0:width] for r in in_refs], axis=0)
    qs[...] = mxu(perm, queries, (1, 0)).astype(bf16)
    os[...] = jnp.zeros_like(os)
    int_copy.wait()

    tall = group * tile_rows
    factors = [scale_ref[0, k] * (log2_e / math.sqrt(dim)) for k in range(heads)]
    short_blocks = max(1, long_blocks // 2)
    long_tokens, short_tokens = long_blocks * tok, short_blocks * tok

    def tile_body(t, _):
        top = scalars[2, t]
        doc = jnp.where(t >= scalars[3, 0], 1, 0)
        at = pl.multiple_of(t * tile_rows, tile_rows)
        spans = jnp.concatenate([lens[pl.ds(at, tile_rows), :]] * group, axis=0)[:, 0:1]
        qt = [
            jnp.concatenate(
                [qs[pl.ds(at, tile_rows), (k * group + g) * dim : (k * group + g + 1) * dim] for g in range(group)],
                axis=0,
            )
            for k in range(heads)
        ]

        def step(blocks_in, first, carry):
            part = min(8, blocks_in)
            cuts = range(0, blocks_in, part)
            ids = [scalars[doc, first + j] for j in range(blocks_in)]
            lane = iota((tall, part * tok), 1)
            scores = [[] for _ in range(heads)]
            for b in cuts:
                keep = lane < spans - (first + b) * tok
                for k in range(heads):
                    keys = jnp.concatenate([kv[n, 0, k] for n in ids[b : b + part]], axis=0)
                    scores[k].append(jnp.where(keep, mxu(qt[k], keys, (1, 1)) * factors[k], -1e30))
            higher, shrink, sums, added = [], [], [None] * heads, [None] * heads
            for k in range(heads):
                most = functools.reduce(jnp.maximum, scores[k])
                higher.append(jnp.maximum(carry[k][0], jnp.max(most, axis=1, keepdims=True)))
                shrink.append(jnp.exp2(carry[k][0] - higher[k]))
            for n, b in enumerate(cuts):
                for k in range(heads):
                    weights = jnp.exp2(scores[k][n] - higher[k])
                    values = jnp.concatenate([kv[n, 1, k] for n in ids[b : b + part]], axis=0)
                    product = mxu(weights.astype(bf16), values, (1, 0))
                    sums[k] = weights if n == 0 else sums[k] + weights
                    added[k] = product if n == 0 else added[k] + product
            return tuple(
                (
                    higher[k],
                    carry[k][1] * shrink[k] + jnp.sum(sums[k], axis=1, keepdims=True),
                    carry[k][2] * shrink[k] + added[k],
                )
                for k in range(heads)
            )

        start = tuple(
            (jnp.full((tall, 1), -1e30, f32), jnp.zeros((tall, 1), f32), jnp.zeros((tall, dim), f32))
            for _ in range(heads)
        )
        longs = (top + (long_tokens - short_tokens - 1)) // long_tokens
        shorts = jnp.where(top > longs * long_tokens, 1, 0)

        @pl.when(top > 0)
        def _():
            done = lax.fori_loop(0, longs, lambda c, carry: step(long_blocks, c * long_blocks, carry), start)
            done = lax.fori_loop(0, shorts, lambda c, carry: step(short_blocks, longs * long_blocks, carry), done)
            for k in range(heads):
                _, denom, acc = done[k]
                out = (acc * (scale_ref[1, k] / denom)).astype(bf16)
                for g in range(group):
                    col = (k * group + g) * dim
                    os[pl.ds(at, tile_rows), col : col + dim] = out[g * tile_rows : (g + 1) * tile_rows]

        return 0

    lax.fori_loop(0, places // tile_rows, tile_body, 0)
    out = mxu(perm, os[...], (0, 0)).astype(bf16)
    for s in range(count):
        out_refs[s][...] = out[s * slots : (s + 1) * slots]
    for copy in copies:
        copy.wait()


def attend(received, kv_codes, kv_scale, later, listed, group):
    count = len(received)
    slots, wide = received[0].shape
    width = wide - lanes
    total = count * slots
    places = total + tile_rows
    got = pl.pallas_call(
        functools.partial(attend_kernel, count, len(later), listed, group, min(32, listed)),
        out_shape=[jax.ShapeDtypeStruct((slots, width), bf16)] * count
        + [pltpu.VMEM(a.shape, a.dtype) for a in later],
        in_specs=[smem()] + [vmem()] * (count + 1) + [hbm()] * len(later),
        out_specs=[vmem()] * (count + len(later)),
        scratch_shapes=[
            pltpu.VMEM((places, width), bf16),
            pltpu.VMEM((places, width), bf16),
            pltpu.VMEM((places, lanes), jnp.int32),
            pltpu.VMEM((8, lanes), jnp.int32),
            pltpu.SMEM((8, lanes), jnp.int32),
            pltpu.SemaphoreType.DMA((max(1, len(later)),)),
            pltpu.SemaphoreType.DMA,
        ],
        compiler_params=pltpu.CompilerParams(vmem_limit_bytes=12 * mib),
        name="attend",
    )(kv_scale, kv_codes, *received, *map(stay, later))
    return got[:count], got[count:]


def project_kernel(count, parts, at_ref, *refs):
    in_refs, w_ref = refs[:count], refs[count]
    own_ref, out_refs = refs[count + 1], refs[count + 2 : count + 1 + parts]
    x, y = refs[count + 1 + parts :]
    rows = in_refs[0].shape[0]
    piece = own_ref.shape[0]

    for s in range(count):
        source = at_ref[0] - s
        source = jnp.where(source < 0, source + count, source)
        x[pl.ds(pl.multiple_of(source * rows, rows), rows), :] = in_refs[s][...]
    cols = w_ref.shape[1]
    wide = 256 if cols % 256 == 0 else cols
    for c in range(0, cols, wide):
        y[:, c : c + wide] = mxu(x[...], w_ref[:, c : c + wide], (1, 0))
    for s in range(parts):
        target = at_ref[1] + s
        target = jnp.where(target >= parts, target - parts, target)
        value = y[pl.ds(pl.multiple_of(target * piece, piece), piece), :]
        if s == 0:
            own_ref[...] = value
        else:
            out_refs[s - 1][...] = value.astype(bf16)


def project(at, pieces, w_out, parts):
    count = len(pieces)
    rows, depth = pieces[0].shape
    cols = w_out.shape[1]
    tall = rows * count
    piece = tall // parts
    got = pl.pallas_call(
        functools.partial(project_kernel, count, parts),
        out_shape=[jax.ShapeDtypeStruct((piece, cols), f32)]
        + [jax.ShapeDtypeStruct((piece, cols), bf16)] * (parts - 1),
        in_specs=[smem()] + [vmem()] * (count + 1),
        out_specs=[vmem()] * parts,
        scratch_shapes=[pltpu.VMEM((tall, depth), bf16), pltpu.VMEM((tall, cols), f32)],
        compiler_params=pltpu.CompilerParams(vmem_limit_bytes=12 * mib),
        name="project",
    )(at, *pieces, w_out)
    return got[0], got[1:]


hidden_tile = 256


def swiglu_kernel(row_devs, head_devs, at_ref, gain_ref, *refs):
    count = row_devs * head_devs
    pieces, refs = refs[:count], refs[count:]
    gate_ref, up_ref, down_ref = refs[:3]
    keep_refs, send_refs = refs[3 : 3 + row_devs], refs[3 + row_devs : 3 + 2 * row_devs]
    x, inner = refs[3 + 2 * row_devs :]
    rows, cols = pieces[0].shape
    tall, hidden = inner.shape
    width = row_devs * cols
    order = [*range(0, head_devs, 2), *range(1, head_devs, 2)]

    def turned(n):
        n = at_ref[0] + n % row_devs
        n = jnp.where(n >= row_devs, n - row_devs, n)
        return pl.multiple_of(n * cols, cols)

    for at, j in enumerate(order):
        values = [pieces[s * head_devs + j][...].astype(f32) for s in range(row_devs)]
        squares = sum(jnp.sum(v * v, axis=1, keepdims=True) for v in values)
        inverse = lax.rsqrt(squares / width + norm_eps)
        for s in range(row_devs):
            value = values[s] * inverse * gain_ref[:, pl.ds(turned(-s), cols)]
            x[s, at * rows : (at + 1) * rows, :] = value.astype(bf16)

    for c in range(0, hidden, hidden_tile):
        cut = slice(c, c + hidden_tile)
        gate = jnp.zeros((tall, hidden_tile), f32)
        up = jnp.zeros((tall, hidden_tile), f32)
        for s in range(row_devs):
            gate = gate + mxu(x[s], gate_ref[pl.ds(turned(-s), cols), cut], (1, 0))
            up = up + mxu(x[s], up_ref[pl.ds(turned(-s), cols), cut], (1, 0))
        inner[:, cut] = (gate / (1.0 + jnp.exp(-gate)) * up).astype(bf16)

    for i in range(row_devs):
        for c in range(0, cols, hidden_tile):
            cut = slice(c, c + hidden_tile)
            y = mxu(inner[...], down_ref[:, pl.ds(pl.multiple_of(turned(i) + c, hidden_tile), hidden_tile)], (1, 0))
            keep_refs[i][:, cut] = y[: tall // 2]
            send_refs[i][:, cut] = y[tall // 2 :].astype(bf16)


def swiglu(at, pieces, gain, w_gate, w_up, w_down, row_devs, head_devs):
    rows, cols = pieces[0].shape
    tall = rows * head_devs
    width, hidden = w_gate.shape
    half = rows * head_devs // 2
    got = pl.pallas_call(
        functools.partial(swiglu_kernel, row_devs, head_devs),
        out_shape=[jax.ShapeDtypeStruct((half, cols), f32)] * row_devs
        + [jax.ShapeDtypeStruct((half, cols), bf16)] * row_devs,
        in_specs=[smem(), vmem()] + [vmem()] * (len(pieces) + 3),
        out_specs=[vmem()] * (2 * row_devs),
        scratch_shapes=[
            pltpu.VMEM((row_devs, tall, cols), bf16),
            pltpu.VMEM((tall, hidden), bf16),
        ],
        compiler_params=pltpu.CompilerParams(vmem_limit_bytes=12 * mib),
        name="swiglu",
    )(at, gain.reshape(1, width), *pieces, w_gate, w_up, w_down)
    return got[:row_devs], got[row_devs:]


def shift(x, axis, step):
    n = lax.axis_size(axis)
    return lax.ppermute(x, axis, [(i, (i + step) % n) for i in range(n)])


def swap(x, axis, flip):
    return lax.ppermute(x, axis, [(i, i ^ flip) for i in range(lax.axis_size(axis))])


def feed_forward(at, hidden_state, norm_gain, w_gate, w_up, w_down):
    row_devs = lax.axis_size("rows")
    head_devs = lax.axis_size("heads")
    rows = hidden_state.shape[0]
    pieces = []
    for s in range(row_devs):
        piece = shift(hidden_state, "rows", s) if s else hidden_state
        across = swap(piece, "heads", 2)
        pieces += [piece, swap(piece, "heads", 1), across, swap(across, "heads", 1)]
    keeps, sends = swiglu(at, pieces, norm_gain, w_gate, w_up, w_down, row_devs, head_devs)
    total = hidden_state.astype(f32)
    order = sorted(range(row_devs), key=lambda i: (i == 0, abs(2 * i - row_devs)))
    for i in order:
        pair = keeps[i] + swap(sends[i], "heads", 1).astype(f32)
        part = pair[:rows] + swap(pair[rows:].astype(bf16), "heads", 2).astype(f32)
        total = total + (shift(part.astype(bf16), "rows", i).astype(f32) if i else part)
    return total.astype(bf16)


def feed_forward_gathered(hidden_state, norm_gain, w_gate, w_up, w_down):
    model_width = norm_gain.shape[0]
    full_rows = lax.all_gather(hidden_state, "rows", axis=1, tiled=True)
    every = lax.all_gather(full_rows, "heads", axis=0, tiled=True).astype(f32)
    totals = jnp.sum(every * every, axis=1)
    normed = (every * lax.rsqrt(totals / model_width + norm_eps)[:, None] * norm_gain).astype(bf16)
    gate = jnp.dot(normed, w_gate, preferred_element_type=f32)
    up = jnp.dot(normed, w_up, preferred_element_type=f32)
    inner = (jax.nn.silu(gate) * up).astype(bf16)
    partial_sum = jnp.dot(inner, w_down, preferred_element_type=f32).astype(bf16)
    section = lax.psum_scatter(partial_sum, "heads", scatter_dimension=0, tiled=True)
    ffn = lax.psum_scatter(section, "rows", scatter_dimension=1, tiled=True)
    return (hidden_state.astype(f32) + ffn.astype(f32)).astype(bf16)


def shards(
    resid, queries, kv_codes, kv_scale, row_blocks, row_len, w_out, norm_gain, w_gate, w_up, w_down
):
    row_devs = lax.axis_size("rows")
    head_devs = lax.axis_size("heads")
    rows_dev, width_q = queries.shape
    listed = row_blocks.shape[1]
    blocks_dev = kv_codes.shape[0]
    heads_dev, head_dim = kv_codes.shape[2], kv_codes.shape[4]
    group = width_q // (heads_dev * head_dim)
    capacity = max(2, 2 * rows_dev // row_devs)
    slots = -(-capacity // 16) * 16
    my_row = lax.axis_index("rows").astype(jnp.int32)
    my_head = lax.axis_index("heads").astype(jnp.int32)
    at = jnp.stack([my_row, my_head])

    place, sends = dispatch(at, queries, row_blocks, row_len, row_devs, slots, blocks_dev)
    received = [sends[0]] + [shift(sends[s], "rows", s) for s in range(1, row_devs)]
    (kv_near,) = fetch(place, kv_codes)
    results, (w_gate, w_out) = attend(received, kv_near, kv_scale, (w_gate, w_out), listed, group)
    back = [results[0]] + [shift(results[s], "rows", -s) for s in range(1, row_devs)]
    attended = jnp.dot(place, jnp.concatenate(back, axis=0), preferred_element_type=f32).astype(bf16)
    pieces = [attended] + [shift(attended, "rows", s) for s in range(1, row_devs)]
    pieces, w_up, w_down = lax.optimization_barrier((pieces, *fetch(attended, w_up, w_down)))
    own, others = project(at, pieces, w_out, head_devs)
    attn_out = own
    for s in range(1, head_devs):
        attn_out = attn_out + shift(others[s - 1], "heads", s).astype(f32)
    hidden_state = (resid.astype(f32) + attn_out).astype(bf16)

    if head_devs == 4 and hidden_state.shape[1] % hidden_tile == 0:
        return feed_forward(at, hidden_state, norm_gain, w_gate, w_up, w_down)
    return feed_forward_gathered(hidden_state, norm_gain, w_gate, w_up, w_down)


def solution(mesh):
    placed = (
        P(("groups", "heads"), "rows"),
        P(("groups", "rows"), "heads"),
        P(("groups", "rows"), None, "heads", None, None),
        P("groups", "heads"),
        P(("groups", "rows"), None),
        P(("groups", "rows")),
        P("heads", "rows"),
        P(),
        P(None, ("rows", "heads")),
        P(None, ("rows", "heads")),
        P(("rows", "heads"), None),
    )
    return jax.shard_map(
        shards,
        mesh=mesh,
        in_specs=placed,
        out_specs=P(("groups", "heads"), "rows"),
        check_vma=False,
    )
```

```python
import functools
import math

import jax
import jax.numpy as jnp
from jax import lax
from jax.experimental import pallas as pl
from jax.experimental.pallas import tpu as pltpu
from jax.sharding import PartitionSpec as P

norm_eps = 1e-06
log2_e = 1.4426950408889634
mib = 1 << 20
lanes = 128
f32 = jnp.float32
bf16 = jnp.bfloat16

vmem = functools.partial(pl.BlockSpec, memory_space=pltpu.VMEM)
smem = functools.partial(pl.BlockSpec, memory_space=pltpu.SMEM)
hbm = functools.partial(pl.BlockSpec, memory_space=pltpu.HBM)


def stay(x):
    return pltpu.with_memory_space_constraint(x, pltpu.HBM)


def iota(shape, dim):
    return lax.broadcasted_iota(jnp.int32, shape, dim)


def mxu(a, b, contract):
    return lax.dot_general(a, b, ((contract[:1], contract[1:]), ((), ())), preferred_element_type=f32)


def fetch_kernel(count, after_ref, *refs):
    sources, targets, sems = refs[:count], refs[count : 2 * count], refs[2 * count]
    copies = [pltpu.make_async_copy(sources[i], targets[i], sems.at[i]) for i in range(count)]
    for copy in copies:
        copy.start()
    for copy in copies:
        copy.wait()


def fetch(after, *arrays):
    count = len(arrays)
    return pl.pallas_call(
        functools.partial(fetch_kernel, count),
        out_shape=[pltpu.VMEM(a.shape, a.dtype) for a in arrays],
        in_specs=[pl.BlockSpec(memory_space=pl.ANY)] + [hbm()] * count,
        out_specs=[vmem()] * count,
        scratch_shapes=[pltpu.SemaphoreType.DMA((count,))],
        cost_estimate=pl.CostEstimate(
            flops=0, bytes_accessed=sum(a.size * a.dtype.itemsize for a in arrays), transcendentals=0
        ),
        compiler_params=pltpu.CompilerParams(vmem_limit_bytes=1 * mib),
        name="fetch",
    )(after, *map(stay, arrays))


def dispatch_kernel(blocks_dev, me_ref, ids_hbm, len_hbm, q_hbm, place_ref, *refs):
    send_refs, (ids_ref, len_ref, q_ref, sems) = refs[:-4], refs[-4:]
    ids_copy = pltpu.make_async_copy(ids_hbm, ids_ref, sems.at[0])
    len_copy = pltpu.make_async_copy(len_hbm, len_ref, sems.at[1])
    q_copy = pltpu.make_async_copy(q_hbm, q_ref, sems.at[2])
    for copy in (ids_copy, len_copy, q_copy):
        copy.start()
    count = len(send_refs)
    slots = send_refs[0].shape[0]
    width = q_ref.shape[1]
    rows, listed = ids_ref.shape
    me = me_ref[0]
    ids_copy.wait()
    len_copy.wait()
    ids = ids_ref[...].astype(f32)
    owner = jnp.floor((ids[:, 0:1] + 0.5) * (1.0 / blocks_dev))
    ahead = owner - me.astype(f32)
    ahead = jnp.where(ahead < 0, ahead + count, ahead)
    lane = iota((rows, lanes), 1)
    hot = jnp.where(lane.astype(f32) == ahead, 1.0, 0.0)
    lower = jnp.where(iota((rows, rows), 1) < iota((rows, rows), 0), 1.0, 0.0)
    before = mxu(lower.astype(bf16), hot.astype(bf16), (1, 0))
    rank = jnp.sum(before * hot, axis=1, keepdims=True)
    target = ahead * slots + rank
    place = jnp.where(iota((rows, count * slots), 1).astype(f32) == target, 1.0, 0.0).astype(bf16)
    place_ref[...] = place
    local = (ids - owner * blocks_dev).astype(bf16)
    eye = jnp.where(iota((listed, lanes), 0) == iota((listed, lanes), 1), 1.0, 0.0).astype(bf16)
    meta = mxu(local, eye, (1, 0))
    spread = jnp.broadcast_to(len_ref[...].astype(f32), (rows, rows))
    length = jnp.sum(
        jnp.where(iota((rows, rows), 0) == iota((rows, rows), 1), spread, 0.0), axis=1, keepdims=True
    )
    high = jnp.floor(length * (1.0 / 64))
    meta = jnp.where(lane == listed, high, meta)
    meta = jnp.where(lane == listed + 1, length - high * 64, meta)
    q_copy.wait()
    send = mxu(place, q_ref[...], (0, 0)).astype(bf16)
    send_meta = mxu(place, meta.astype(bf16), (0, 0)).astype(bf16)
    for s in range(count):
        send_refs[s][:, 0:width] = send[s * slots : (s + 1) * slots]
        send_refs[s][:, width : width + lanes] = send_meta[s * slots : (s + 1) * slots]


def dispatch(me, queries, row_blocks, row_len, count, slots, blocks_dev):
    rows, width = queries.shape
    outs = [jax.ShapeDtypeStruct((rows, count * slots), bf16)]
    outs += [jax.ShapeDtypeStruct((slots, width + lanes), bf16)] * count
    got = pl.pallas_call(
        functools.partial(dispatch_kernel, blocks_dev),
        out_shape=outs,
        in_specs=[smem(), hbm(), hbm(), hbm()],
        out_specs=[vmem()] * (count + 1),
        scratch_shapes=[
            pltpu.VMEM(row_blocks.shape, jnp.int32),
            pltpu.VMEM((1, rows), jnp.int32),
            pltpu.VMEM((rows, width), bf16),
            pltpu.SemaphoreType.DMA((3,)),
        ],
        compiler_params=pltpu.CompilerParams(vmem_limit_bytes=8 * mib),
        name="dispatch",
    )(me, stay(row_blocks), stay(row_len.reshape(1, rows)), stay(queries))
    return got[0], got[1:]


tile_rows = 16


def attend_kernel(count, later, listed, group, long_blocks, scale_ref, kv, *refs):
    in_refs, refs = refs[:count], refs[count:]
    later_refs, refs = refs[:later], refs[later:]
    out_refs, refs = refs[:count], refs[count:]
    later_outs, refs = refs[:later], refs[later:]
    qs, os, lens, ints, scalars, later_sems, int_sem = refs
    copies = [pltpu.make_async_copy(later_refs[i], later_outs[i], later_sems.at[i]) for i in range(later)]
    for copy in copies:
        copy.start()
    slots = out_refs[0].shape[0]
    width = out_refs[0].shape[1]
    total = count * slots
    places = qs.shape[0]
    heads, tok, dim = kv.shape[2:]
    meta = jnp.concatenate([r[:, width : width + lanes] for r in in_refs], axis=0).astype(f32)
    lane = iota((total, lanes), 1)
    length = jnp.sum(
        jnp.where(lane == listed, meta * 64.0, jnp.where(lane == listed + 1, meta, 0.0)), axis=1, keepdims=True
    )
    ids = jnp.where(lane < listed, meta, 0.0)
    slot = iota((total, 1), 0).astype(f32)
    valid = length > 0.0
    big = float(total)

    def first_list(mask):
        first = jnp.min(jnp.where(mask, slot, big), axis=0, keepdims=True)
        return jnp.sum(jnp.where(slot == first, ids, 0.0), axis=0, keepdims=True)

    list_a = first_list(valid)
    same_a = jnp.sum(jnp.abs(ids - list_a), axis=1, keepdims=True) == 0.0
    in_a = valid & same_a
    in_b = valid & jnp.logical_not(same_a)
    list_b = first_list(in_b)
    span = float(2 * listed * tok)
    key = jnp.where(in_a, 2 * span + length, jnp.where(in_b, span + length, 0.0))
    key = key * total + (total - 1 - slot)
    eye = iota((total, total), 0) == iota((total, total), 1)
    key_row = jnp.sum(jnp.where(eye, key, 0.0), axis=0, keepdims=True)
    len_row = jnp.sum(jnp.where(eye, length, 0.0), axis=0, keepdims=True)
    rank = jnp.sum(jnp.where(key > key_row, 1.0, 0.0), axis=0, keepdims=True)
    a_row = key_row >= 2 * span * total
    b_row = jnp.logical_and(key_row >= span * total, jnp.logical_not(a_row))
    a_count = jnp.sum(jnp.where(a_row, 1.0, 0.0), axis=1, keepdims=True)
    a_tiles = jnp.floor((a_count + (tile_rows - 1)) * (1.0 / tile_rows))
    spot = jnp.where(a_row, rank, jnp.where(b_row, rank - a_count + a_tiles * tile_rows, float(places)))
    placed = iota((places, total), 0).astype(f32) == spot
    perm = jnp.where(placed, 1.0, 0.0).astype(bf16)
    len_sorted = jnp.sum(jnp.where(placed, len_row, 0.0), axis=1, keepdims=True)
    lens[...] = jnp.broadcast_to(len_sorted, (places, lanes)).astype(jnp.int32)
    tops = jnp.sum(
        jnp.where(iota((places, lanes), 0) == iota((places, lanes), 1) * tile_rows, len_sorted, 0.0),
        axis=0,
        keepdims=True,
    )
    row = iota((8, lanes), 0)
    ints[...] = jnp.where(
        row == 0, list_a, jnp.where(row == 1, list_b, jnp.where(row == 2, tops, a_tiles))
    ).astype(jnp.int32)
    int_copy = pltpu.make_async_copy(ints, scalars, int_sem)
    int_copy.start()
    queries = jnp.concatenate([r[:, 0:width] for r in in_refs], axis=0)
    qs[...] = mxu(perm, queries, (1, 0)).astype(bf16)
    os[...] = jnp.zeros_like(os)
    int_copy.wait()

    tall = group * tile_rows
    factors = [scale_ref[0, k] * (log2_e / math.sqrt(dim)) for k in range(heads)]
    short_blocks = max(1, long_blocks // 2)
    long_tokens, short_tokens = long_blocks * tok, short_blocks * tok

    def tile_body(t, _):
        top = scalars[2, t]
        doc = jnp.where(t >= scalars[3, 0], 1, 0)
        at = pl.multiple_of(t * tile_rows, tile_rows)
        spans = jnp.concatenate([lens[pl.ds(at, tile_rows), :]] * group, axis=0)[:, 0:1]
        qt = [
            jnp.concatenate(
                [qs[pl.ds(at, tile_rows), (k * group + g) * dim : (k * group + g + 1) * dim] for g in range(group)],
                axis=0,
            )
            for k in range(heads)
        ]

        def step(blocks_in, first, carry):
            part = min(8, blocks_in)
            cuts = range(0, blocks_in, part)
            ids = [scalars[doc, first + j] for j in range(blocks_in)]
            lane = iota((tall, part * tok), 1)
            scores = [[] for _ in range(heads)]
            for b in cuts:
                keep = lane < spans - (first + b) * tok
                for k in range(heads):
                    keys = jnp.concatenate([kv[n, 0, k] for n in ids[b : b + part]], axis=0)
                    scores[k].append(jnp.where(keep, mxu(qt[k], keys, (1, 1)) * factors[k], -1e30))
            higher, shrink, sums, added = [], [], [None] * heads, [None] * heads
            for k in range(heads):
                most = functools.reduce(jnp.maximum, scores[k])
                higher.append(jnp.maximum(carry[k][0], jnp.max(most, axis=1, keepdims=True)))
                shrink.append(jnp.exp2(carry[k][0] - higher[k]))
            for n, b in enumerate(cuts):
                for k in range(heads):
                    weights = jnp.exp2(scores[k][n] - higher[k])
                    values = jnp.concatenate([kv[n, 1, k] for n in ids[b : b + part]], axis=0)
                    product = mxu(weights.astype(bf16), values, (1, 0))
                    sums[k] = weights if n == 0 else sums[k] + weights
                    added[k] = product if n == 0 else added[k] + product
            return tuple(
                (
                    higher[k],
                    carry[k][1] * shrink[k] + jnp.sum(sums[k], axis=1, keepdims=True),
                    carry[k][2] * shrink[k] + added[k],
                )
                for k in range(heads)
            )

        start = tuple(
            (jnp.full((tall, 1), -1e30, f32), jnp.zeros((tall, 1), f32), jnp.zeros((tall, dim), f32))
            for _ in range(heads)
        )
        longs = (top + (long_tokens - short_tokens - 1)) // long_tokens
        shorts = jnp.where(top > longs * long_tokens, 1, 0)

        @pl.when(top > 0)
        def _():
            done = lax.fori_loop(0, longs, lambda c, carry: step(long_blocks, c * long_blocks, carry), start)
            done = lax.fori_loop(0, shorts, lambda c, carry: step(short_blocks, longs * long_blocks, carry), done)
            for k in range(heads):
                _, denom, acc = done[k]
                out = (acc * (scale_ref[1, k] / denom)).astype(bf16)
                for g in range(group):
                    col = (k * group + g) * dim
                    os[pl.ds(at, tile_rows), col : col + dim] = out[g * tile_rows : (g + 1) * tile_rows]

        return 0

    lax.fori_loop(0, places // tile_rows, tile_body, 0)
    out = mxu(perm, os[...], (0, 0)).astype(bf16)
    for s in range(count):
        out_refs[s][...] = out[s * slots : (s + 1) * slots]
    for copy in copies:
        copy.wait()


def attend(received, kv_codes, kv_scale, later, listed, group):
    count = len(received)
    slots, wide = received[0].shape
    width = wide - lanes
    total = count * slots
    places = total + tile_rows
    got = pl.pallas_call(
        functools.partial(attend_kernel, count, len(later), listed, group, min(32, listed)),
        out_shape=[jax.ShapeDtypeStruct((slots, width), bf16)] * count
        + [pltpu.VMEM(a.shape, a.dtype) for a in later],
        in_specs=[smem()] + [vmem()] * (count + 1) + [hbm()] * len(later),
        out_specs=[vmem()] * (count + len(later)),
        scratch_shapes=[
            pltpu.VMEM((places, width), bf16),
            pltpu.VMEM((places, width), bf16),
            pltpu.VMEM((places, lanes), jnp.int32),
            pltpu.VMEM((8, lanes), jnp.int32),
            pltpu.SMEM((8, lanes), jnp.int32),
            pltpu.SemaphoreType.DMA((max(1, len(later)),)),
            pltpu.SemaphoreType.DMA,
        ],
        compiler_params=pltpu.CompilerParams(vmem_limit_bytes=12 * mib),
        name="attend",
    )(kv_scale, kv_codes, *received, *map(stay, later))
    return got[:count], got[count:]


def project_kernel(count, parts, at_ref, *refs):
    in_refs, w_ref = refs[:count], refs[count]
    own_ref, out_refs = refs[count + 1], refs[count + 2 : count + 1 + parts]
    x, y = refs[count + 1 + parts :]
    rows = in_refs[0].shape[0]
    piece = own_ref.shape[0]

    for s in range(count):
        source = at_ref[0] - s
        source = jnp.where(source < 0, source + count, source)
        x[pl.ds(pl.multiple_of(source * rows, rows), rows), :] = in_refs[s][...]
    cols = w_ref.shape[1]
    wide = 256 if cols % 256 == 0 else cols
    for c in range(0, cols, wide):
        y[:, c : c + wide] = mxu(x[...], w_ref[:, c : c + wide], (1, 0))
    for s in range(parts):
        target = at_ref[1] + s
        target = jnp.where(target >= parts, target - parts, target)
        value = y[pl.ds(pl.multiple_of(target * piece, piece), piece), :]
        if s == 0:
            own_ref[...] = value
        else:
            out_refs[s - 1][...] = value.astype(bf16)


def project(at, pieces, w_out, parts):
    count = len(pieces)
    rows, depth = pieces[0].shape
    cols = w_out.shape[1]
    tall = rows * count
    piece = tall // parts
    got = pl.pallas_call(
        functools.partial(project_kernel, count, parts),
        out_shape=[jax.ShapeDtypeStruct((piece, cols), f32)]
        + [jax.ShapeDtypeStruct((piece, cols), bf16)] * (parts - 1),
        in_specs=[smem()] + [vmem()] * (count + 1),
        out_specs=[vmem()] * parts,
        scratch_shapes=[pltpu.VMEM((tall, depth), bf16), pltpu.VMEM((tall, cols), f32)],
        compiler_params=pltpu.CompilerParams(vmem_limit_bytes=12 * mib),
        name="project",
    )(at, *pieces, w_out)
    return got[0], got[1:]


hidden_tile = 256


def swiglu_kernel(row_devs, head_devs, at_ref, gain_ref, *refs):
    count = row_devs * head_devs
    pieces, refs = refs[:count], refs[count:]
    gate_ref, up_ref, down_ref = refs[:3]
    keep_refs, send_refs = refs[3 : 3 + row_devs], refs[3 + row_devs : 3 + 2 * row_devs]
    x, inner = refs[3 + 2 * row_devs :]
    rows, cols = pieces[0].shape
    tall, hidden = inner.shape
    width = row_devs * cols
    order = [*range(0, head_devs, 2), *range(1, head_devs, 2)]

    def turned(n):
        n = at_ref[0] + n % row_devs
        n = jnp.where(n >= row_devs, n - row_devs, n)
        return pl.multiple_of(n * cols, cols)

    for at, j in enumerate(order):
        values = [pieces[s * head_devs + j][...].astype(f32) for s in range(row_devs)]
        squares = sum(jnp.sum(v * v, axis=1, keepdims=True) for v in values)
        inverse = lax.rsqrt(squares / width + norm_eps)
        for s in range(row_devs):
            value = values[s] * inverse * gain_ref[:, pl.ds(turned(-s), cols)]
            x[s, at * rows : (at + 1) * rows, :] = value.astype(bf16)

    for c in range(0, hidden, hidden_tile):
        cut = slice(c, c + hidden_tile)
        gate = jnp.zeros((tall, hidden_tile), f32)
        up = jnp.zeros((tall, hidden_tile), f32)
        for s in range(row_devs):
            gate = gate + mxu(x[s], gate_ref[pl.ds(turned(-s), cols), cut], (1, 0))
            up = up + mxu(x[s], up_ref[pl.ds(turned(-s), cols), cut], (1, 0))
        inner[:, cut] = (gate / (1.0 + jnp.exp(-gate)) * up).astype(bf16)

    for i in range(row_devs):
        for c in range(0, cols, hidden_tile):
            cut = slice(c, c + hidden_tile)
            y = mxu(inner[...], down_ref[:, pl.ds(pl.multiple_of(turned(i) + c, hidden_tile), hidden_tile)], (1, 0))
            keep_refs[i][:, cut] = y[: tall // 2]
            send_refs[i][:, cut] = y[tall // 2 :].astype(bf16)


def swiglu(at, pieces, gain, w_gate, w_up, w_down, row_devs, head_devs):
    rows, cols = pieces[0].shape
    tall = rows * head_devs
    width, hidden = w_gate.shape
    half = rows * head_devs // 2
    got = pl.pallas_call(
        functools.partial(swiglu_kernel, row_devs, head_devs),
        out_shape=[jax.ShapeDtypeStruct((half, cols), f32)] * row_devs
        + [jax.ShapeDtypeStruct((half, cols), bf16)] * row_devs,
        in_specs=[smem(), vmem()] + [vmem()] * (len(pieces) + 3),
        out_specs=[vmem()] * (2 * row_devs),
        scratch_shapes=[
            pltpu.VMEM((row_devs, tall, cols), bf16),
            pltpu.VMEM((tall, hidden), bf16),
        ],
        compiler_params=pltpu.CompilerParams(vmem_limit_bytes=12 * mib),
        name="swiglu",
    )(at, gain.reshape(1, width), *pieces, w_gate, w_up, w_down)
    return got[:row_devs], got[row_devs:]


def shift(x, axis, step):
    n = lax.axis_size(axis)
    return lax.ppermute(x, axis, [(i, (i + step) % n) for i in range(n)])


def swap(x, axis, flip):
    return lax.ppermute(x, axis, [(i, i ^ flip) for i in range(lax.axis_size(axis))])


def feed_forward(at, hidden_state, norm_gain, w_gate, w_up, w_down):
    row_devs = lax.axis_size("rows")
    head_devs = lax.axis_size("heads")
    rows = hidden_state.shape[0]
    pieces = []
    for s in range(row_devs):
        piece = shift(hidden_state, "rows", s) if s else hidden_state
        across = swap(piece, "heads", 2)
        pieces += [piece, swap(piece, "heads", 1), across, swap(across, "heads", 1)]
    keeps, sends = swiglu(at, pieces, norm_gain, w_gate, w_up, w_down, row_devs, head_devs)
    total = hidden_state.astype(f32)
    order = sorted(range(row_devs), key=lambda i: (i == 0, abs(2 * i - row_devs)))
    for i in order:
        got = swap(sends[i], "heads", 1)
        across = (keeps[i][rows:] + got[rows:].astype(f32)).astype(bf16)
        part = keeps[i][:rows] + got[:rows].astype(f32) + swap(across, "heads", 2).astype(f32)
        total = total + (shift(part.astype(bf16), "rows", i).astype(f32) if i else part)
    return total.astype(bf16)


def feed_forward_gathered(hidden_state, norm_gain, w_gate, w_up, w_down):
    model_width = norm_gain.shape[0]
    full_rows = lax.all_gather(hidden_state, "rows", axis=1, tiled=True)
    every = lax.all_gather(full_rows, "heads", axis=0, tiled=True).astype(f32)
    totals = jnp.sum(every * every, axis=1)
    normed = (every * lax.rsqrt(totals / model_width + norm_eps)[:, None] * norm_gain).astype(bf16)
    gate = jnp.dot(normed, w_gate, preferred_element_type=f32)
    up = jnp.dot(normed, w_up, preferred_element_type=f32)
    inner = (jax.nn.silu(gate) * up).astype(bf16)
    partial_sum = jnp.dot(inner, w_down, preferred_element_type=f32).astype(bf16)
    section = lax.psum_scatter(partial_sum, "heads", scatter_dimension=0, tiled=True)
    ffn = lax.psum_scatter(section, "rows", scatter_dimension=1, tiled=True)
    return (hidden_state.astype(f32) + ffn.astype(f32)).astype(bf16)


def shards(
    resid, queries, kv_codes, kv_scale, row_blocks, row_len, w_out, norm_gain, w_gate, w_up, w_down
):
    row_devs = lax.axis_size("rows")
    head_devs = lax.axis_size("heads")
    rows_dev, width_q = queries.shape
    listed = row_blocks.shape[1]
    blocks_dev = kv_codes.shape[0]
    heads_dev, head_dim = kv_codes.shape[2], kv_codes.shape[4]
    group = width_q // (heads_dev * head_dim)
    capacity = max(2, 2 * rows_dev // row_devs)
    slots = -(-capacity // 16) * 16
    my_row = lax.axis_index("rows").astype(jnp.int32)
    my_head = lax.axis_index("heads").astype(jnp.int32)
    at = jnp.stack([my_row, my_head])

    place, sends = dispatch(at, queries, row_blocks, row_len, row_devs, slots, blocks_dev)
    received = [sends[0]] + [shift(sends[s], "rows", s) for s in range(1, row_devs)]
    (kv_near,) = fetch(place, kv_codes)
    results, (w_gate, w_out) = attend(received, kv_near, kv_scale, (w_gate, w_out), listed, group)
    back = [results[0]] + [shift(results[s], "rows", -s) for s in range(1, row_devs)]
    attended = jnp.dot(place, jnp.concatenate(back, axis=0), preferred_element_type=f32).astype(bf16)
    pieces = [attended] + [shift(attended, "rows", s) for s in range(1, row_devs)]
    pieces, w_up, w_down = lax.optimization_barrier((pieces, *fetch(attended, w_up, w_down)))
    own, others = project(at, pieces, w_out, head_devs)
    attn_out = own
    for s in range(1, head_devs):
        attn_out = attn_out + shift(others[s - 1], "heads", s).astype(f32)
    hidden_state = (resid.astype(f32) + attn_out).astype(bf16)

    if head_devs == 4 and hidden_state.shape[1] % hidden_tile == 0:
        return feed_forward(at, hidden_state, norm_gain, w_gate, w_up, w_down)
    return feed_forward_gathered(hidden_state, norm_gain, w_gate, w_up, w_down)


def solution(mesh):
    placed = (
        P(("groups", "heads"), "rows"),
        P(("groups", "rows"), "heads"),
        P(("groups", "rows"), None, "heads", None, None),
        P("groups", "heads"),
        P(("groups", "rows"), None),
        P(("groups", "rows")),
        P("heads", "rows"),
        P(),
        P(None, ("rows", "heads")),
        P(None, ("rows", "heads")),
        P(("rows", "heads"), None),
    )
    return jax.shard_map(
        shards,
        mesh=mesh,
        in_specs=placed,
        out_specs=P(("groups", "heads"), "rows"),
        check_vma=False,
    )
```
